512 devices in a mesh: seq: 256 (over x, z, y_hi, core), sub: 2 (over y_lo).
Axes of the slice: x: 4, y: 4 (y_hi: 2, y_lo: 2; y = y_hi * 2 + y_lo), z: 16, core: 2. Of those that a mesh axis runs over, the one named last changes fastest.
Arguments:
- query_input: bfloat16 [65536, 2048], P(('seq', 'sub')), may hold values from -400 to 400
- key_input: bfloat16 [65536, 1024], P(('seq', 'sub')), may hold values from -400 to 400
- saved_value_input: bfloat16 [65536, 1024], P(('seq', 'sub')), may hold values from -6 to 6
- grad_output: bfloat16 [65536, 2048], P(('seq', 'sub')), may hold values from -16 to 16
- query_gain: float32 [128], replicated, may hold values from 0.5 to 1.5
- key_gain: float32 [128], replicated, may hold values from 0.5 to 1.5
Outputs:
- grad_query: bfloat16 [65536, 2048], P(('seq', 'sub'))
- grad_key: bfloat16 [65536, 1024], P(('seq', 'sub'))
- grad_value: bfloat16 [65536, 1024], P(('seq', 'sub'))
- grad_query_gain: float32 [128], replicated
- grad_key_gain: float32 [128], replicated
The draws below stay inside these ranges and needn't reach their ends.
All inputs are finite; a program needn't handle non-finite values.
Results may differ from the reference program's by a relative error of at most 0.014.
Values may be sent and summed in bfloat16 or wider, within the bound.
A program may use at most 64 MiB of HBM per device.

```python
import jax
import jax.numpy as jnp
from jax import lax

HQ = 16
KEY_VALUE_HEADS = 8
HEAD_SIZE = 128
WIN = 512
TOK_DEV = 128
NHALO = 4
DOCUMENT_TOKENS = 65536


def rescaled_row_block(key, row_count, column_count):
    leading_key_index, second_key, third_key = jax.random.split(key, 3)
    column_scale = 10.0 ** jax.random.uniform(third_key, (1, column_count))
    base_values = jnp.clip(jax.random.normal(leading_key_index, (row_count, column_count)), -4.0, 4.0)
    row_scale = 10.0 ** jax.random.uniform(second_key, (row_count, 1))
    return base_values * row_scale * column_scale


def draw_query_input(key, part):
    return rescaled_row_block(jax.random.fold_in(key, 11), DOCUMENT_TOKENS, HQ * HEAD_SIZE).astype(jnp.bfloat16)


def draw_key_input(key, part):
    return rescaled_row_block(jax.random.fold_in(key, 12), DOCUMENT_TOKENS, KEY_VALUE_HEADS * HEAD_SIZE).astype(jnp.bfloat16)


def draw_grad_output(key, part):
    leading_key_index = jax.random.fold_in(key, 13)
    position_ramp = (jnp.arange(DOCUMENT_TOKENS).astype(jnp.float32) / (DOCUMENT_TOKENS - 1))[:, None]
    base_values = jnp.clip(jax.random.normal(leading_key_index, (DOCUMENT_TOKENS, HQ * HEAD_SIZE)), -4.0, 4.0)
    position_ramp = 1.0 + 2.0 * position_ramp
    return (base_values * position_ramp).astype(jnp.bfloat16)


def level_of(key, extent, cuts, least, top_value):
    gain = 1.0
    for position, shards_of in cuts:
        heights = jax.random.uniform(jax.random.fold_in(jax.random.fold_in(key, 6), position), (shards_of,), jnp.float32, least / len(cuts), top_value / len(cuts))
        gain = gain * jnp.repeat(jnp.exp(heights), extent[position] // shards_of).reshape((-1,) + (1,) * (len(extent) - 1 - position))
    return gain


def gaussian(own_key, dims, spread, most, shards=(), dtype=jnp.bfloat16):
    array = spread * jax.random.normal(own_key, dims, jnp.float32)
    if shards:
        array = array * level_of(own_key, dims, shards, -0.22, 0.18)
    return jnp.clip(array, -most, most).astype(dtype)


def setup_inputs(seed: int = 0) -> dict:
    streams_of = jax.random.split(jax.random.key(seed), 7)
    return {
        "query_input": draw_query_input(jax.random.fold_in(streams_of[6], 71), 0),
        "key_input": draw_key_input(jax.random.fold_in(streams_of[6], 71), 0),
        "saved_value_input": gaussian(streams_of[2], (DOCUMENT_TOKENS, KEY_VALUE_HEADS * HEAD_SIZE), 1.0, 6.0, ((0, 512),)),
        "grad_output": draw_grad_output(jax.random.fold_in(streams_of[6], 71), 0),
        "query_gain": jnp.clip(1.0 + 0.1 * jax.random.normal(streams_of[4], (HEAD_SIZE,), jnp.float32), 0.5, 1.5),
        "key_gain": jnp.clip(1.0 + 0.1 * jax.random.normal(streams_of[5], (HEAD_SIZE,), jnp.float32), 0.5, 1.5),
    }


epsilon = 1e-06
score_scale = 168.0 ** (-0.5)

def rope_tables(positions, half_width):
    frequency = 10000.0 ** (-jnp.arange(half_width).astype(jnp.float32) / half_width)
    angles = positions[:, None] * frequency[None, :]
    return (jnp.cos(angles), jnp.sin(angles))

def rotate(values, cosine_table, sine_table):
    half_width = values.shape[-1] // 2
    leading = values[..., :half_width]
    trailing = values[..., half_width:]
    cosine_wide = cosine_table[:, None, :]
    sine_wide = sine_table[:, None, :]
    return jnp.concatenate([leading * cosine_wide - trailing * sine_wide, trailing * cosine_wide + leading * sine_wide], axis=-1)

def prepare(raw_rows, gain_vector, cosine_table, sine_table):
    head_dim = gain_vector.shape[0]
    values = raw_rows.astype(jnp.float32).reshape(raw_rows.shape[0], -1, head_dim)
    inverse = lax.rsqrt(lax.optimization_barrier(jnp.mean(values * values, axis=-1, keepdims=True)) + epsilon)
    unit_rows = values * inverse
    prepared = rotate(unit_rows * gain_vector, cosine_table, sine_table).astype(jnp.bfloat16)
    return (prepared.reshape(raw_rows.shape), unit_rows, inverse)

def norm_back(grad_rotated, unit_rows, inverse, gain_vector, cosine_table, sine_table):
    grad_scaled = rotate(grad_rotated, cosine_table, -sine_table)
    gain_term = lax.optimization_barrier(jnp.sum(grad_scaled * unit_rows, axis=(0, 1)))
    grad_unit = grad_scaled * gain_vector
    grad_raw = (grad_unit - unit_rows * lax.optimization_barrier(jnp.mean(grad_unit * unit_rows, axis=-1, keepdims=True))) * inverse
    return (grad_raw.reshape(grad_raw.shape[0], -1).astype(jnp.bfloat16), gain_term)

def attend_block(query_ready, key_pairs, grad_block, admitted, query_heads, key_heads, head_dim):
    row_count = query_ready.shape[0]
    key_span = key_pairs.shape[1]
    group_size = query_heads // key_heads
    queries = query_ready.astype(jnp.float32).reshape(row_count, key_heads, group_size, head_dim)
    grads = grad_block.astype(jnp.float32).reshape(row_count, key_heads, group_size, head_dim)
    key_rows = key_pairs[0].astype(jnp.float32).reshape(key_span, key_heads, head_dim)
    value_rows = key_pairs[1].astype(jnp.float32).reshape(key_span, key_heads, head_dim)
    scores = jnp.einsum('ikgd,jkd->kgij', queries, key_rows) * score_scale
    weights = jnp.where(admitted, jnp.exp(scores), 0.0)
    probabilities = weights / lax.optimization_barrier(jnp.sum(weights, axis=-1, keepdims=True))
    weights_low = lax.optimization_barrier(probabilities.astype(jnp.bfloat16)).astype(jnp.float32)
    grad_values = jnp.einsum('kgij,ikgd->jkd', weights_low, grads)
    grad_probs = jnp.einsum('ikgd,jkd->kgij', grads, value_rows)
    row_inner = lax.optimization_barrier(jnp.sum(probabilities * grad_probs, axis=-1, keepdims=True))
    grad_scores = (probabilities * (grad_probs - row_inner) * score_scale).astype(jnp.bfloat16)
    grad_scores = lax.optimization_barrier(grad_scores).astype(jnp.float32)
    grad_queries = jnp.einsum('kgij,jkd->ikgd', grad_scores, key_rows).reshape(row_count, query_heads, head_dim)
    grad_keys = jnp.einsum('kgij,ikgd->jkd', grad_scores, queries).reshape(key_span, key_heads * head_dim)
    return (grad_queries, jnp.stack([grad_keys, grad_values.reshape(key_span, key_heads * head_dim)]))

def reference(query_input, key_input, saved_value_input, grad_output, query_gain, key_gain):
    head_dim = query_gain.shape[0]
    query_heads = query_input.shape[1] // head_dim
    key_heads = key_input.shape[1] // head_dim
    width_keys = key_input.shape[1]
    token_count_total = query_input.shape[0]
    shard_count = token_count_total // TOK_DEV
    key_span = (NHALO + 1) * TOK_DEV
    cosine_all, sine_all = rope_tables(jnp.arange(token_count_total).astype(jnp.float32), head_dim // 2)
    key_ready = prepare(key_input, key_gain, cosine_all, sine_all)[0]
    padding = jnp.zeros((2, NHALO * TOK_DEV, width_keys), jnp.bfloat16)
    pairs_padded = jnp.concatenate([padding, jnp.stack([key_ready, saved_value_input])], axis=1)
    offsets_grid = jnp.arange(TOK_DEV)[:, None] - jnp.arange(key_span)[None, :] + NHALO * TOK_DEV

    def finish_keys(finished_index, accumulated):
        begin_row = (jnp.maximum(finished_index, 0) * TOK_DEV).astype(jnp.int32)
        raw_rows = lax.dynamic_slice_in_dim(key_input, begin_row, TOK_DEV, 0)
        cosine_block = lax.dynamic_slice_in_dim(cosine_all, begin_row, TOK_DEV, 0)
        sine_block = lax.dynamic_slice_in_dim(sine_all, begin_row, TOK_DEV, 0)
        prepared_parts = prepare(raw_rows, key_gain, cosine_block, sine_block)
        grad_raw, gain_term = norm_back(accumulated[0].reshape(TOK_DEV, key_heads, head_dim), prepared_parts[1], prepared_parts[2], key_gain, cosine_block, sine_block)
        return (grad_raw, accumulated[1].astype(jnp.bfloat16), gain_term)

    def advance(state_carry, shard_index):
        pending, query_total, key_total = state_carry
        begin_row = (shard_index * TOK_DEV).astype(jnp.int32)
        query_rows = lax.dynamic_slice_in_dim(query_input, begin_row, TOK_DEV, 0)
        grad_rows = lax.dynamic_slice_in_dim(grad_output, begin_row, TOK_DEV, 0)
        cosine_block = lax.dynamic_slice_in_dim(cosine_all, begin_row, TOK_DEV, 0)
        sine_block = lax.dynamic_slice_in_dim(sine_all, begin_row, TOK_DEV, 0)
        query_ready, query_unit, query_inverse = prepare(query_rows, query_gain, cosine_block, sine_block)
        key_rows = lax.dynamic_slice_in_dim(pairs_padded, begin_row, key_span, 1)
        key_positions = begin_row - NHALO * TOK_DEV + jnp.arange(key_span)
        admitted = (offsets_grid >= 0) & (offsets_grid < WIN) & (key_positions[None, :] >= 0)
        grad_rotated, grad_pairs = attend_block(query_ready, key_rows, grad_rows, admitted, query_heads, key_heads, head_dim)
        grad_query_rows, query_term = norm_back(grad_rotated, query_unit, query_inverse, query_gain, cosine_block, sine_block)
        remote = grad_pairs[:, :NHALO * TOK_DEV].reshape(2, NHALO, TOK_DEV, width_keys)
        remote = jnp.moveaxis(remote, 1, 0)
        own_part = grad_pairs[:, NHALO * TOK_DEV:][None]
        blank = jnp.zeros((1, 2, TOK_DEV, width_keys), jnp.float32)
        combined = jnp.concatenate([pending, blank], axis=0) + jnp.concatenate([remote, own_part], axis=0)
        grad_key_rows, grad_value_rows, key_term = finish_keys(shard_index - NHALO, combined[0])
        return ((combined[1:], query_total + query_term, key_total + key_term), (grad_query_rows, grad_key_rows, grad_value_rows))
    initial = (jnp.zeros((NHALO, 2, TOK_DEV, width_keys), jnp.float32), jnp.zeros((head_dim,), jnp.float32), jnp.zeros((head_dim,), jnp.float32))
    final_carry, outputs = lax.scan(advance, initial, jnp.arange(shard_count).astype(jnp.int32))
    pending, query_total, key_total = final_carry
    grad_query = outputs[0].reshape(token_count_total, -1)
    key_parts = [outputs[1][NHALO:]]
    value_parts = [outputs[2][NHALO:]]
    for slot_index in range(NHALO):
        grad_key_rows, grad_value_rows, key_term = finish_keys(jnp.int32(shard_count - NHALO + slot_index), pending[slot_index])
        key_parts.append(grad_key_rows[None])
        value_parts.append(grad_value_rows[None])
        key_total = key_total + key_term
    grad_key = jnp.concatenate(key_parts, axis=0).reshape(token_count_total, -1)
    grad_value = jnp.concatenate(value_parts, axis=0).reshape(token_count_total, -1)
    return (grad_query, grad_key, grad_value, query_total, key_total)
```

```python
import functools

import jax
import jax.numpy as jnp
import numpy as np
from jax import lax
from jax.experimental import pallas as pl
from jax.experimental.pallas import tpu as pltpu
from jax.sharding import PartitionSpec as P

MESH = pl.DeviceIdType.MESH
T = 128
D = 128
NP = 8
NH = 4
NZ = 16
NX = 4
EPS = 1e-6
SCALE = 168.0 ** (-0.5)
LOG2E = 1.4426950408889634
LN2 = 0.6931471805599453
F32 = jnp.float32
BF16 = jnp.bfloat16


def device(col, y, c):
    return ((col * 2 + y // 2) * 2 + c, y % 2)


def place(y, c):
    return 4 * (y // 2) + 2 * c + y % 2


def rows_of(block):
    return pl.ds(pl.multiple_of(block * T, T), T)


def cols_of(start, size):
    return pl.ds(pl.multiple_of(start, 128), size)


def unit_of(raw):
    inverse = lax.rsqrt(jnp.mean(raw * raw, axis=-1, keepdims=True) + EPS)
    return raw * inverse, inverse


def rope(rows, cosine, sine):
    return rows * cosine + pltpu.roll(rows, 64, 1) * sine


def rope_back(rows, cosine, sine):
    return rows * cosine - pltpu.roll(rows, 64, 1) * sine


def dot_nt(a, b):
    return lax.dot_general(a, b, (((1,), (1,)), ((), ())), preferred_element_type=F32)


def dot_nn(a, b):
    return jnp.dot(a, b, preferred_element_type=F32)


def kernel(
    q_in,
    k_in,
    v_in,
    g_in,
    qgain_ref,
    kgain_ref,
    freq_ref,
    dq_out,
    dk_out,
    dv_out,
    qterm_out,
    kterm_out,
    st_kv,
    st_qg,
    kv,
    qg,
    kready,
    ktrans,
    ctab,
    stab,
    weights,
    gprobs,
    dkv,
    dq_res,
    dkv_res,
    halo_res,
    halo_ret,
    plane_q,
    plane_kv,
    terms,
    ar_a,
    ar_b,
    ar_c,
    core_send,
    core_recv,
    kv_send,
    kv_recv,
    qg_send,
    qg_recv,
    halo_send,
    halo_recv,
    ret_send,
    ret_recv,
    dq_send,
    dq_recv,
    dkv_send,
    dkv_recv,
    out_send,
    out_recv,
    out_local,
    ara_send,
    ara_recv,
    arb_send,
    arb_recv,
    arc_send,
    arc_recv,
):
    s = lax.axis_index("seq")
    c = s % 2
    col = s // 4
    y = 2 * ((s // 2) % 2) + lax.axis_index("sub")
    z = col % NZ
    x = col // NZ
    other = 1 - c
    mine = place(y, c)
    theirs = place(y, other)
    partner = device(col, y, other)
    after = device((col + 1) % (NX * NZ), y, c)
    before = device((col + NX * NZ - 1) % (NX * NZ), y, c)

    column_peers = [(dy, dc) for dy in range(4) for dc in range(2) if (dy, dc) != (0, 0)]

    def column_device(dy, dc):
        return device(col, (y + dy) % 4, (c + dc) % 2)

    def z_device(dz):
        return device(x * NZ + (z + dz) % NZ, y, c)

    def x_device(dx):
        return device(((x + dx) % NX) * NZ + z, y, c)

    barrier = pltpu.get_barrier_semaphore()
    greeted = [column_device(dy, dc) for dy, dc in column_peers]
    greeted += [after, before]
    greeted += [z_device(dz) for dz in range(1, NZ)]
    greeted += [x_device(dx) for dx in range(1, NX)]
    for target in greeted:
        pl.semaphore_signal(barrier, inc=1, device_id=target, device_id_type=MESH)
    pl.semaphore_wait(barrier, len(greeted))

    def remote(src, dst, send, recv, target):
        return pltpu.make_async_remote_copy(
            src_ref=src, dst_ref=dst, send_sem=send, recv_sem=recv, device_id=target, device_id_type=MESH
        )

    sends = []

    core_copies = []
    for i, (ref, width) in enumerate(((k_in, 4 * D), (v_in, 4 * D), (q_in, 8 * D), (g_in, 8 * D))):
        stage = st_kv.at[i] if i < 2 else st_qg.at[i - 2]
        core_copies.append(
            remote(ref.at[:, cols_of(other * width, width)], stage, core_send.at[i], core_recv.at[i], partner)
        )

    def spread(kind, sources, width, slots, first_row_block, send, recv, block, turn):
        for i, source in enumerate(sources):
            base, ref = source
            for dy in range(1, 4):
                yy = (y + dy) % 4
                copy = remote(
                    ref.at[:, cols_of(base + yy * width, width)],
                    slots.at[i, rows_of(first_row_block + block)],
                    send.at[turn, i, dy],
                    recv.at[i, block],
                    device(col, yy, c),
                )
                copy.start()
                sends.append(copy)
            pltpu.make_async_copy(
                ref.at[:, cols_of(base + y * width, width)],
                slots.at[i, rows_of(first_row_block + block)],
                recv.at[i, block],
            ).start()

    core_copies[0].start()
    core_copies[1].start()
    own_kv = [(c * 4 * D, k_in), (c * 4 * D, v_in)]
    spread("kv", own_kv, D, kv, NH, kv_send, kv_recv, mine, 0)
    core_copies[2].start()
    core_copies[3].start()
    core_copies[0].wait_recv()
    core_copies[1].wait_recv()
    spread("kv", [(0, st_kv.at[0]), (0, st_kv.at[1])], D, kv, NH, kv_send, kv_recv, theirs, 1)
    own_qg = [(c * 8 * D, q_in), (c * 8 * D, g_in)]
    spread("qg", own_qg, 2 * D, qg, 0, qg_send, qg_recv, mine, 0)
    core_copies[2].wait_recv()
    core_copies[3].wait_recv()
    spread("qg", [(0, st_qg.at[0]), (0, st_qg.at[1])], 2 * D, qg, 0, qg_send, qg_recv, theirs, 1)

    first_token = col * (NP * T) - NH * T
    half = (NP + NH) * T // 2
    step_rows = 64

    @pl.loop(0, half // step_rows)
    def _(step):
        row = lax.broadcasted_iota(jnp.int32, (step_rows, D), 0)
        lane = lax.broadcasted_iota(jnp.int32, (step_rows, D), 1)
        low = lane < 64
        token = first_token + step * step_rows + row + jnp.where(low, 0, half)
        angle = token.astype(F32) * freq_ref[...]
        cosine = jnp.cos(angle)
        sine = jnp.sin(angle)
        cosine_turned = pltpu.roll(cosine, 64, 1)
        sine_turned = pltpu.roll(sine, 64, 1)
        near = pl.ds(pl.multiple_of(step * step_rows, step_rows), step_rows)
        far = pl.ds(pl.multiple_of(half + step * step_rows, step_rows), step_rows)
        ctab[near] = jnp.where(low, cosine, cosine_turned)
        ctab[far] = jnp.where(low, cosine_turned, cosine)
        stab[near] = jnp.where(low, -sine, sine_turned)
        stab[far] = jnp.where(low, -sine_turned, sine)

    dkv[...] = jnp.zeros_like(dkv)
    terms[...] = jnp.zeros_like(terms)
    kgain = kgain_ref[...]
    qgain = qgain_ref[...]

    def wait_kv(block):
        for i in range(2):
            slot = kv.at[i, rows_of(NH + block)]
            pltpu.make_async_copy(slot, slot, kv_recv.at[i, block]).wait()

    def halo_copy(i):
        return remote(
            kv.at[:, rows_of(NP + i)], kv.at[:, rows_of(i)], halo_send.at[i], halo_recv.at[i], after
        )

    def prepare_keys(block):
        rows = rows_of(block)
        unit, _ = unit_of(kv[0, rows].astype(F32))
        turned = rope(unit * kgain, ctab[rows], stab[rows])
        kready[rows] = turned.astype(BF16)
        ktrans[block] = turned.T.astype(BF16)

    @pl.loop(0, NH)
    def _(i):
        wait_kv(NH + i)
        halo_copy(i).start()

    @pl.loop(0, NH)
    def _(i):
        wait_kv(i)

    @pl.loop(NH, NH + NP)
    def _(block):
        prepare_keys(block)

    halo_valid = jnp.where(col == 0, 0.0, 1.0)
    key_row = lax.broadcasted_iota(jnp.int32, (T, 2 * T), 0)
    query_lane = lax.broadcasted_iota(jnp.int32, (T, 2 * T), 1) % T
    newer = key_row > query_lane

    def norm_back(turned_grad, raw, gain, cosine, sine):
        unit, inverse = unit_of(raw)
        w = rope_back(turned_grad, cosine, sine)
        term = jnp.sum(w * unit, axis=0, keepdims=True)
        grad_unit = w * gain
        grad = (grad_unit - unit * jnp.mean(grad_unit * unit, axis=-1, keepdims=True)) * inverse
        return grad.astype(BF16), term

    def owner(block):
        return 2 * (block // 4) + block % 2, (block // 2) % 2

    def dq_copies(block):
        yy, cc = owner(block)
        src = dq_res.at[block]
        dst = plane_q.at[cc, :, cols_of(y * 2 * D, 2 * D)]
        return (
            remote(src, dst, dq_send.at[block], dq_recv.at[y, cc], device(col, yy, c)),
            pltpu.make_async_copy(src, dst, dq_recv.at[y, cc]),
            yy,
        )

    def dkv_copies(block):
        yy, cc = owner(block)
        src = dkv_res.at[block]
        dst = plane_kv.at[cc, :, :, cols_of(y * D, D)]
        return (
            remote(src, dst, dkv_send.at[block], dkv_recv.at[y, cc], device(col, yy, c)),
            pltpu.make_async_copy(src, dst, dkv_recv.at[y, cc]),
            yy,
        )

    def give(copies):
        far, near, yy = copies

        @pl.when(yy == y)
        def _():
            near.start()

        @pl.when(yy != y)
        def _():
            far.start()

    def attend(block):
        rows = rows_of(block)
        for i in range(2):
            slot = qg.at[i, rows]
            pltpu.make_async_copy(slot, slot, qg_recv.at[i, block]).wait()
        own = rows_of(block + NH)
        cosine, sine = ctab[own], stab[own]
        raw = [qg[0, rows, h * D : (h + 1) * D].astype(F32) for h in range(2)]
        queries = jnp.concatenate(
            [(rope(unit_of(r)[0] * qgain, cosine, sine) * (SCALE * LOG2E)).astype(BF16) for r in raw], axis=0
        )
        grads = jnp.concatenate([qg[1, rows, h * D : (h + 1) * D] for h in range(2)], axis=0)
        total = jnp.zeros((1, 2 * T), F32)
        inner = jnp.zeros((1, 2 * T), F32)
        for t in range(NH + 1):
            keys = rows_of(block + t)
            weight = jnp.exp2(dot_nt(kready[keys], queries))
            if t == 0:
                weight = jnp.where(newer, weight, 0.0)
            if t == NH:
                weight = jnp.where(newer, 0.0, weight)
            else:
                weight = weight * jnp.where(block + t < NH, halo_valid, 1.0)
            grad_prob = dot_nt(kv[1, keys], grads)
            total = total + jnp.sum(weight, axis=0, keepdims=True)
            inner = inner + jnp.sum(weight * grad_prob, axis=0, keepdims=True)
            weights[t] = weight
            gprobs[t] = grad_prob
        inverse = 1.0 / total
        inner = inner * inverse
        grad_query = jnp.zeros((D, 2 * T), F32)
        for t in range(NH + 1):
            keys = rows_of(block + t)
            prob = weights[t] * inverse
            grad_score = (prob * (gprobs[t] - inner)).astype(BF16)
            dkv[1, keys] += dot_nn(prob.astype(BF16), grads)
            dkv[0, keys] += dot_nn(grad_score, queries)
            grad_query = grad_query + dot_nn(ktrans[block + t], grad_score)
        for h in range(2):
            turned = grad_query[:, h * T : (h + 1) * T].T * SCALE
            grad, term = norm_back(turned, raw[h], qgain, cosine, sine)
            dq_res[block, :, h * D : (h + 1) * D] = grad
            terms[0:1] += term
        give(dq_copies(block))

    @pl.loop(NH, NP)
    def _(block):
        attend(block)

    @pl.loop(0, NH)
    def _(i):
        halo_copy(i).wait_recv()
        prepare_keys(i)

    def return_copy(i):
        return remote(halo_res.at[i], halo_ret.at[i], ret_send.at[i], ret_recv.at[i], before)

    @pl.loop(0, NH)
    def _(block):
        attend(block)
        keys = rows_of(block)
        grad_key = dkv[0, keys] * LN2
        halo_res[block, 0] = grad_key.astype(BF16)
        halo_res[block, 1] = dkv[1, keys].astype(BF16)
        return_copy(block).start()
        unit, _ = unit_of(kv[0, keys].astype(F32))
        w = rope_back(grad_key, ctab[keys], stab[keys])
        terms[1:2] += jnp.sum(w * unit, axis=0, keepdims=True)

    @pl.loop(0, NH)
    def _(block):
        keys = rows_of(block + NH)
        grad, term = norm_back(dkv[0, keys] * LN2, kv[0, keys].astype(F32), kgain, ctab[keys], stab[keys])
        dkv_res[block, 0] = grad
        dkv_res[block, 1] = dkv[1, keys].astype(BF16)
        terms[1:2] += term
        give(dkv_copies(block))

    @pl.loop(NH, NP)
    def _(block):
        keys = rows_of(block + NH)
        unit, _ = unit_of(kv[0, keys].astype(F32))
        w = rope_back(dkv[0, keys] * LN2, ctab[keys], stab[keys])
        terms[1:2] += jnp.sum(w * unit, axis=0, keepdims=True)

    ar_a[mine] = terms[...]
    stage_a = [
        remote(terms, ar_a.at[mine], ara_send.at[i], ara_recv.at[mine], column_device(dy, dc))
        for i, (dy, dc) in enumerate(column_peers)
    ]
    for copy in stage_a:
        copy.start()
    for dy, dc in column_peers:
        slot = place((y + dy) % 4, (c + dc) % 2)
        pltpu.make_async_copy(ar_a.at[slot], ar_a.at[slot], ara_recv.at[slot]).wait()
    ar_b[z] = jnp.sum(ar_a[...], axis=0)
    stage_b = [
        remote(ar_b.at[z], ar_b.at[z], arb_send.at[dz], arb_recv.at[z], z_device(dz)) for dz in range(1, NZ)
    ]
    for copy in stage_b:
        copy.start()
    for dz in range(1, NZ):
        slot = (z + dz) % NZ
        pltpu.make_async_copy(ar_b.at[slot], ar_b.at[slot], arb_recv.at[slot]).wait()
    ar_c[x] = jnp.sum(ar_b[...], axis=0)
    stage_c = [
        remote(ar_c.at[x], ar_c.at[x], arc_send.at[dx], arc_recv.at[x], x_device(dx)) for dx in range(1, NX)
    ]
    for copy in stage_c:
        copy.start()

    @pl.loop(NH, NP)
    def _(block):
        return_copy(block - NH).wait_recv()
        keys = rows_of(block + NH)
        grad_key = dkv[0, keys] * LN2 + halo_ret[block - NH, 0].astype(F32)
        grad, _ = norm_back(grad_key, kv[0, keys].astype(F32), kgain, ctab[keys], stab[keys])
        dkv_res[block, 0] = grad
        dkv_res[block, 1] = (dkv[1, keys] + halo_ret[block - NH, 1].astype(F32)).astype(BF16)
        give(dkv_copies(block))

    wide, narrow = cols_of(c * 8 * D, 8 * D), cols_of(c * 4 * D, 4 * D)
    plane_parts = (
        (lambda cc: plane_q.at[cc], dq_out.at[:, wide]),
        (lambda cc: plane_kv.at[cc, 0], dk_out.at[:, narrow]),
        (lambda cc: plane_kv.at[cc, 1], dv_out.at[:, narrow]),
    )
    out_copies = []
    for i, (part, target) in enumerate(plane_parts):
        if i < 2:
            for cc in range(2):
                for yy in range(4):
                    if i == 0:
                        slot = plane_q.at[cc, :, cols_of(yy * 2 * D, 2 * D)]
                        sem = dq_recv.at[yy, cc]
                    else:
                        slot = plane_kv.at[cc, :, :, cols_of(yy * D, D)]
                        sem = dkv_recv.at[yy, cc]
                    pltpu.make_async_copy(slot, slot, sem).wait()
        away = remote(part(other), target, out_send.at[i], out_recv.at[i], partner)
        stay = pltpu.make_async_copy(part(c), target, out_local.at[i])
        away.start()
        stay.start()
        out_copies.append((away, stay))

    for dx in range(1, NX):
        slot = (x + dx) % NX
        pltpu.make_async_copy(ar_c.at[slot], ar_c.at[slot], arc_recv.at[slot]).wait()
    gains = jnp.sum(ar_c[...], axis=0)
    qterm_out[...] = gains[0:1]
    kterm_out[...] = gains[1:2]

    for copy in core_copies + sends + stage_a + stage_b + stage_c:
        copy.wait_send()

    @pl.loop(0, NH)
    def _(i):
        halo_copy(i).wait_send()
        return_copy(i).wait_send()

    @pl.loop(0, NP)
    def _(block):
        yy, _ = owner(block)

        @pl.when(yy != y)
        def _():
            dq_copies(block)[0].wait_send()
            dkv_copies(block)[0].wait_send()

    for away, stay in out_copies:
        away.wait()
        stay.wait()


def per_device(query_input, key_input, saved_value_input, grad_output, query_gain, key_gain):
    frequency = (10000.0 ** (-np.arange(64, dtype=np.float64) / 64)).astype(np.float32)
    frequency = jnp.asarray(np.concatenate([frequency, frequency])[None, :])
    anywhere = pl.BlockSpec(memory_space=pl.ANY)
    vmem = pl.BlockSpec(memory_space=pltpu.VMEM)
    dma = pltpu.SemaphoreType.DMA
    span = (NP + NH) * T
    dq, dk, dv, qterm, kterm = pl.pallas_call(
        kernel,
        out_shape=(
            jax.ShapeDtypeStruct((T, 16 * D), BF16),
            jax.ShapeDtypeStruct((T, 8 * D), BF16),
            jax.ShapeDtypeStruct((T, 8 * D), BF16),
            jax.ShapeDtypeStruct((1, D), F32),
            jax.ShapeDtypeStruct((1, D), F32),
        ),
        in_specs=[anywhere] * 4 + [vmem] * 3,
        out_specs=(anywhere, anywhere, anywhere, vmem, vmem),
        scratch_shapes=[
            pltpu.VMEM((2, T, 4 * D), BF16),
            pltpu.VMEM((2, T, 8 * D), BF16),
            pltpu.VMEM((2, span, D), BF16),
            pltpu.VMEM((2, NP * T, 2 * D), BF16),
            pltpu.VMEM((span, D), BF16),
            pltpu.VMEM((NP + NH, D, T), BF16),
            pltpu.VMEM((span, D), F32),
            pltpu.VMEM((span, D), F32),
            pltpu.VMEM((NH + 1, T, 2 * T), F32),
            pltpu.VMEM((NH + 1, T, 2 * T), F32),
            pltpu.VMEM((2, span, D), F32),
            pltpu.VMEM((NP, T, 2 * D), BF16),
            pltpu.VMEM((NP, 2, T, D), BF16),
            pltpu.VMEM((NH, 2, T, D), BF16),
            pltpu.VMEM((NH, 2, T, D), BF16),
            pltpu.VMEM((2, T, 8 * D), BF16),
            pltpu.VMEM((2, 2, T, 4 * D), BF16),
            pltpu.VMEM((8, D), F32),
            pltpu.VMEM((NP, 8, D), F32),
            pltpu.VMEM((NZ, 8, D), F32),
            pltpu.VMEM((NX, 8, D), F32),
            dma((4,)),
            dma((4,)),
            dma((2, 2, 4)),
            dma((2, NP)),
            dma((2, 2, 4)),
            dma((2, NP)),
            dma((NH,)),
            dma((NH,)),
            dma((NH,)),
            dma((NH,)),
            dma((NP,)),
            dma((4, 2)),
            dma((NP,)),
            dma((4, 2)),
            dma((3,)),
            dma((3,)),
            dma((3,)),
            dma((NP,)),
            dma((NP,)),
            dma((NZ,)),
            dma((NZ,)),
            dma((NX,)),
            dma((NX,)),
        ],
        compiler_params=pltpu.CompilerParams(
            collective_id=0, has_side_effects=True, vmem_limit_bytes=40 * 2**20
        ),
        cost_estimate=pl.CostEstimate(flops=1700000000, bytes_accessed=3000000, transcendentals=1400000),
    )(
        query_input,
        key_input,
        saved_value_input,
        grad_output,
        query_gain.reshape(1, D),
        key_gain.reshape(1, D),
        frequency,
    )
    return dq, dk, dv, qterm.reshape(D), kterm.reshape(D)


def solution(mesh):
    tokens = P(("seq", "sub"), None)
    return jax.shard_map(
        per_device,
        mesh=mesh,
        in_specs=(tokens, tokens, tokens, tokens, P(), P()),
        out_specs=(tokens, tokens, tokens, P(), P()),
        check_vma=False,
    )
```

```python
import functools

import jax
import jax.numpy as jnp
import numpy as np
from jax import lax
from jax.experimental import pallas as pl
from jax.experimental.pallas import tpu as pltpu
from jax.sharding import PartitionSpec as P

MESH = pl.DeviceIdType.MESH
T = 128
D = 128
NP = 8
NH = 4
NZ = 16
NX = 4
EPS = 1e-6
SCALE = 168.0 ** (-0.5)
LOG2E = 1.4426950408889634
LN2 = 0.6931471805599453
F32 = jnp.float32
BF16 = jnp.bfloat16


def device(col, y, c):
    return ((col * 2 + y // 2) * 2 + c, y % 2)


def place(y, c):
    return 4 * (y // 2) + 2 * c + y % 2


def rows_of(block):
    return pl.ds(pl.multiple_of(block * T, T), T)


def cols_of(start, size):
    return pl.ds(pl.multiple_of(start, 128), size)


def unit_of(raw):
    inverse = lax.rsqrt(jnp.mean(raw * raw, axis=-1, keepdims=True) + EPS)
    return raw * inverse, inverse


def rope(rows, cosine, sine):
    return rows * cosine + pltpu.roll(rows, 64, 1) * sine


def rope_back(rows, cosine, sine):
    return rows * cosine - pltpu.roll(rows, 64, 1) * sine


def dot_nt(a, b):
    return lax.dot_general(a, b, (((1,), (1,)), ((), ())), preferred_element_type=F32)


def dot_nn(a, b):
    return jnp.dot(a, b, preferred_element_type=F32)


def kernel(
    q_in,
    k_in,
    v_in,
    g_in,
    qgain_in,
    kgain_in,
    freq_in,
    dq_out,
    dk_out,
    dv_out,
    qterm_out,
    kterm_out,
    qgain_ref,
    kgain_ref,
    freq_ref,
    st_kv,
    st_qg,
    kv,
    qg,
    kready,
    ktrans,
    ctab,
    stab,
    weights,
    gprobs,
    dkv,
    dq_res,
    dkv_res,
    halo_res,
    halo_ret,
    plane_q,
    plane_kv,
    terms,
    ar_a,
    ar_b,
    ar_c,
    core_send,
    core_recv,
    kv_send,
    kv_recv,
    qg_send,
    qg_recv,
    halo_send,
    halo_recv,
    ret_send,
    ret_recv,
    dq_send,
    dq_recv,
    dkv_send,
    dkv_recv,
    out_send,
    out_recv,
    out_local,
    ara_send,
    ara_recv,
    arb_send,
    arb_recv,
    arc_send,
    arc_recv,
    small_sem,
    relay_up,
    relay_one,
    relay_two,
    relay_four,
):
    s = lax.axis_index("seq")
    c = s % 2
    col = s // 4
    y = 2 * ((s // 2) % 2) + lax.axis_index("sub")
    z = col % NZ
    x = col // NZ
    other = 1 - c
    mine = place(y, c)
    theirs = place(y, other)
    partner = device(col, y, other)
    after = device((col + 1) % (NX * NZ), y, c)
    before = device((col + NX * NZ - 1) % (NX * NZ), y, c)

    column_peers = [(dy, dc) for dy in range(4) for dc in range(2) if (dy, dc) != (0, 0)]

    def column_device(dy, dc):
        return device(col, (y + dy) % 4, (c + dc) % 2)

    def z_device(dz):
        return device(x * NZ + (z + dz) % NZ, y, c)

    def x_device(dx):
        return device(((x + dx) % NX) * NZ + z, y, c)

    def greet(semaphore, target):
        pl.semaphore_signal(semaphore, inc=1, device_id=target, device_id_type=MESH)

    def load_small(i):
        src, dst = ((qgain_in, qgain_ref), (kgain_in, kgain_ref), (freq_in, freq_ref))[i]
        return pltpu.make_async_copy(src, dst, small_sem.at[i])

    for i in range(3):
        load_small(i).start()

    barrier = pltpu.get_barrier_semaphore()
    greeted = [column_device(dy, dc) for dy, dc in column_peers]
    greeted += [before, z_device(NZ - 1), x_device(NX - 1)]
    for target in greeted:
        greet(barrier, target)
    pl.semaphore_wait(barrier, len(greeted))
    greet(relay_up, z_device(1))
    greet(relay_up, x_device(1))

    def remote(src, dst, send, recv, target):
        return pltpu.make_async_remote_copy(
            src_ref=src, dst_ref=dst, send_sem=send, recv_sem=recv, device_id=target, device_id_type=MESH
        )

    sends = []

    core_copies = []
    for i, (ref, width) in enumerate(((k_in, 4 * D), (v_in, 4 * D), (q_in, 8 * D), (g_in, 8 * D))):
        stage = st_kv.at[i] if i < 2 else st_qg.at[i - 2]
        core_copies.append(
            remote(ref.at[:, cols_of(other * width, width)], stage, core_send.at[i], core_recv.at[i], partner)
        )

    def spread(kind, sources, width, slots, first_row_block, send, recv, block, turn):
        for i, source in enumerate(sources):
            base, ref = source
            for dy in range(1, 4):
                yy = (y + dy) % 4
                copy = remote(
                    ref.at[:, cols_of(base + yy * width, width)],
                    slots.at[i, rows_of(first_row_block + block)],
                    send.at[turn, i, dy],
                    recv.at[i, block],
                    device(col, yy, c),
                )
                copy.start()
                sends.append(copy)
            pltpu.make_async_copy(
                ref.at[:, cols_of(base + y * width, width)],
                slots.at[i, rows_of(first_row_block + block)],
                recv.at[i, block],
            ).start()

    core_copies[0].start()
    core_copies[1].start()
    own_kv = [(c * 4 * D, k_in), (c * 4 * D, v_in)]
    spread("kv", own_kv, D, kv, NH, kv_send, kv_recv, mine, 0)
    core_copies[2].start()
    core_copies[3].start()
    core_copies[0].wait_recv()
    core_copies[1].wait_recv()
    spread("kv", [(0, st_kv.at[0]), (0, st_kv.at[1])], D, kv, NH, kv_send, kv_recv, theirs, 1)
    own_qg = [(c * 8 * D, q_in), (c * 8 * D, g_in)]
    spread("qg", own_qg, 2 * D, qg, 0, qg_send, qg_recv, mine, 0)
    core_copies[2].wait_recv()
    core_copies[3].wait_recv()
    spread("qg", [(0, st_qg.at[0]), (0, st_qg.at[1])], 2 * D, qg, 0, qg_send, qg_recv, theirs, 1)

    for i in range(3):
        load_small(i).wait()

    first_token = col * (NP * T) - NH * T
    half = (NP + NH) * T // 2
    step_rows = 64

    @pl.loop(0, half // step_rows)
    def _(step):
        row = lax.broadcasted_iota(jnp.int32, (step_rows, D), 0)
        lane = lax.broadcasted_iota(jnp.int32, (step_rows, D), 1)
        low = lane < 64
        token = first_token + step * step_rows + row + jnp.where(low, 0, half)
        angle = token.astype(F32) * freq_ref[...]
        cosine = jnp.cos(angle)
        sine = jnp.sin(angle)
        cosine_turned = pltpu.roll(cosine, 64, 1)
        sine_turned = pltpu.roll(sine, 64, 1)
        near = pl.ds(pl.multiple_of(step * step_rows, step_rows), step_rows)
        far = pl.ds(pl.multiple_of(half + step * step_rows, step_rows), step_rows)
        ctab[near] = jnp.where(low, cosine, cosine_turned)
        ctab[far] = jnp.where(low, cosine_turned, cosine)
        stab[near] = jnp.where(low, -sine, sine_turned)
        stab[far] = jnp.where(low, -sine_turned, sine)

    dkv[...] = jnp.zeros_like(dkv)
    terms[...] = jnp.zeros_like(terms)
    kgain = kgain_ref[...]
    qgain = qgain_ref[...]

    def wait_kv(block):
        for i in range(2):
            slot = kv.at[i, rows_of(NH + block)]
            pltpu.make_async_copy(slot, slot, kv_recv.at[i, block]).wait()

    def halo_copy(i):
        return remote(
            kv.at[:, rows_of(NP + i)], kv.at[:, rows_of(i)], halo_send.at[i], halo_recv.at[i], after
        )

    def prepare_keys(block):
        rows = rows_of(block)
        unit, _ = unit_of(kv[0, rows].astype(F32))
        turned = rope(unit * kgain, ctab[rows], stab[rows])
        kready[rows] = turned.astype(BF16)
        ktrans[block] = turned.T.astype(BF16)

    @pl.loop(0, NH)
    def _(i):
        wait_kv(NH + i)
        halo_copy(i).start()

    pl.semaphore_wait(relay_up, 2)
    for target in (z_device(1), z_device(NZ - 1), x_device(1), x_device(NX - 1)):
        greet(relay_one, target)

    @pl.loop(0, NH)
    def _(i):
        wait_kv(i)

    @pl.loop(NH, NH + NP)
    def _(block):
        prepare_keys(block)

    pl.semaphore_wait(relay_one, 4)
    greet(relay_two, z_device(2))
    greet(relay_two, z_device(NZ - 2))

    halo_valid = jnp.where(col == 0, 0.0, 1.0)
    key_row = lax.broadcasted_iota(jnp.int32, (T, 2 * T), 0)
    query_lane = lax.broadcasted_iota(jnp.int32, (T, 2 * T), 1) % T
    newer = key_row > query_lane

    def norm_back(turned_grad, raw, gain, cosine, sine):
        unit, inverse = unit_of(raw)
        w = rope_back(turned_grad, cosine, sine)
        term = jnp.sum(w * unit, axis=0, keepdims=True)
        grad_unit = w * gain
        grad = (grad_unit - unit * jnp.mean(grad_unit * unit, axis=-1, keepdims=True)) * inverse
        return grad.astype(BF16), term

    def owner(block):
        return 2 * (block // 4) + block % 2, (block // 2) % 2

    def dq_parts(block):
        yy, cc = owner(block)
        return dq_res.at[block], plane_q.at[cc, :, cols_of(y * 2 * D, 2 * D)], dq_send.at[block], dq_recv.at[y, cc], yy

    def dkv_parts(block):
        yy, cc = owner(block)
        return dkv_res.at[block], plane_kv.at[cc, :, :, cols_of(y * D, D)], dkv_send.at[block], dkv_recv.at[y, cc], yy

    def give(parts):
        src, dst, send, recv, yy = parts

        @pl.when(yy == y)
        def _():
            pltpu.make_async_copy(src, dst, recv).start()

        @pl.when(yy != y)
        def _():
            remote(src, dst, send, recv, device(col, yy, c)).start()

    def given(parts):
        src, dst, send, recv, yy = parts

        @pl.when(yy != y)
        def _():
            remote(src, dst, send, recv, device(col, yy, c)).wait_send()

    def attend(block):
        rows = rows_of(block)
        for i in range(2):
            slot = qg.at[i, rows]
            pltpu.make_async_copy(slot, slot, qg_recv.at[i, block]).wait()
        own = rows_of(block + NH)
        cosine, sine = ctab[own], stab[own]
        raw = [qg[0, rows, h * D : (h + 1) * D].astype(F32) for h in range(2)]
        queries = jnp.concatenate(
            [(rope(unit_of(r)[0] * qgain, cosine, sine) * (SCALE * LOG2E)).astype(BF16) for r in raw], axis=0
        )
        grads = jnp.concatenate([qg[1, rows, h * D : (h + 1) * D] for h in range(2)], axis=0)
        total = jnp.zeros((1, 2 * T), F32)
        inner = jnp.zeros((1, 2 * T), F32)
        for t in range(NH + 1):
            keys = rows_of(block + t)
            weight = jnp.exp2(dot_nt(kready[keys], queries))
            if t == 0:
                weight = jnp.where(newer, weight, 0.0)
            if t == NH:
                weight = jnp.where(newer, 0.0, weight)
            else:
                weight = weight * jnp.where(block + t < NH, halo_valid, 1.0)
            grad_prob = dot_nt(kv[1, keys], grads)
            total = total + jnp.sum(weight, axis=0, keepdims=True)
            inner = inner + jnp.sum(weight * grad_prob, axis=0, keepdims=True)
            weights[t] = weight
            gprobs[t] = grad_prob
        inverse = 1.0 / total
        inner = inner * inverse
        grad_query = jnp.zeros((D, 2 * T), F32)
        for t in range(NH + 1):
            keys = rows_of(block + t)
            prob = weights[t] * inverse
            grad_score = (prob * (gprobs[t] - inner)).astype(BF16)
            dkv[1, keys] += dot_nn(prob.astype(BF16), grads)
            dkv[0, keys] += dot_nn(grad_score, queries)
            grad_query = grad_query + dot_nn(ktrans[block + t], grad_score)
        for h in range(2):
            turned = grad_query[:, h * T : (h + 1) * T].T * SCALE
            grad, term = norm_back(turned, raw[h], qgain, cosine, sine)
            dq_res[block, :, h * D : (h + 1) * D] = grad
            terms[0:1] += term

    def in_turn(i):
        pair = i // 2
        core = pair // 2 + c - 2 * (pair // 2) * c
        return 4 * (1 - pair % 2) + 2 * core + i % 2

    @pl.loop(0, 2)
    def _(i):
        attend(in_turn(i))

    @pl.loop(0, NH)
    def _(i):
        halo_copy(i).wait_recv()
        prepare_keys(i)

    pl.semaphore_wait(relay_two, 2)
    greet(relay_four, z_device(4))
    greet(relay_four, z_device(NZ - 4))

    @pl.loop(2, NP)
    def _(i):
        attend(in_turn(i))

    def return_copy(i):
        return remote(halo_res.at[i], halo_ret.at[i], ret_send.at[i], ret_recv.at[i], before)

    @pl.loop(0, NH)
    def _(block):
        keys = rows_of(block)
        halo_res[block, 0] = (dkv[0, keys] * LN2).astype(BF16)
        halo_res[block, 1] = dkv[1, keys].astype(BF16)
        return_copy(block).start()

    @pl.loop(0, NH + NP)
    def _(block):
        keys = rows_of(block)
        unit, _ = unit_of(kv[0, keys].astype(F32))
        w = rope_back(dkv[0, keys] * LN2, ctab[keys], stab[keys])
        terms[1:2] += jnp.sum(w * unit, axis=0, keepdims=True)

    ar_a[mine] = terms[...]
    stage_a = [
        remote(terms, ar_a.at[mine], ara_send.at[i], ara_recv.at[mine], column_device(dy, dc))
        for i, (dy, dc) in enumerate(column_peers)
    ]
    for copy in stage_a:
        copy.start()

    @pl.loop(0, NP)
    def _(block):
        give(dq_parts(block))

    for dy, dc in column_peers:
        slot = place((y + dy) % 4, (c + dc) % 2)
        pltpu.make_async_copy(ar_a.at[slot], ar_a.at[slot], ara_recv.at[slot]).wait()
    ar_c[x] = jnp.sum(ar_a[...], axis=0)
    stage_c = [
        remote(ar_c.at[x], ar_c.at[x], arc_send.at[dx], arc_recv.at[x], x_device(dx)) for dx in range(1, NX)
    ]
    for copy in stage_c:
        copy.start()

    @pl.loop(0, NH)
    def _(block):
        keys = rows_of(block + NH)
        grad, _ = norm_back(dkv[0, keys] * LN2, kv[0, keys].astype(F32), kgain, ctab[keys], stab[keys])
        dkv_res[block, 0] = grad
        dkv_res[block, 1] = dkv[1, keys].astype(BF16)
        give(dkv_parts(block))

    pl.semaphore_wait(relay_four, 2)
    for dx in range(1, NX):
        slot = (x + dx) % NX
        pltpu.make_async_copy(ar_c.at[slot], ar_c.at[slot], arc_recv.at[slot]).wait()
    ar_b[z] = jnp.sum(ar_c[...], axis=0)
    stage_b = [
        remote(ar_b.at[z], ar_b.at[z], arb_send.at[dz], arb_recv.at[z], z_device(dz)) for dz in range(1, NZ)
    ]
    for copy in stage_b:
        copy.start()

    @pl.loop(NH, NP)
    def _(block):
        return_copy(block - NH).wait_recv()
        keys = rows_of(block + NH)
        grad_key = dkv[0, keys] * LN2 + halo_ret[block - NH, 0].astype(F32)
        grad, _ = norm_back(grad_key, kv[0, keys].astype(F32), kgain, ctab[keys], stab[keys])
        dkv_res[block, 0] = grad
        dkv_res[block, 1] = (dkv[1, keys] + halo_ret[block - NH, 1].astype(F32)).astype(BF16)
        give(dkv_parts(block))

    wide, narrow = cols_of(c * 8 * D, 8 * D), cols_of(c * 4 * D, 4 * D)
    plane_parts = (
        (lambda cc: plane_q.at[cc], dq_out.at[:, wide]),
        (lambda cc: plane_kv.at[cc, 0], dk_out.at[:, narrow]),
        (lambda cc: plane_kv.at[cc, 1], dv_out.at[:, narrow]),
    )
    out_copies = []
    for i, (part, target) in enumerate(plane_parts):
        if i < 2:
            for cc in range(2):
                for yy in range(4):
                    if i == 0:
                        slot = plane_q.at[cc, :, cols_of(yy * 2 * D, 2 * D)]
                        sem = dq_recv.at[yy, cc]
                    else:
                        slot = plane_kv.at[cc, :, :, cols_of(yy * D, D)]
                        sem = dkv_recv.at[yy, cc]
                    pltpu.make_async_copy(slot, slot, sem).wait()
        away = remote(part(other), target, out_send.at[i], out_recv.at[i], partner)
        stay = pltpu.make_async_copy(part(c), target, out_local.at[i])
        away.start()
        stay.start()
        out_copies.append((away, stay))

    for copy in core_copies + sends + stage_a + stage_b + stage_c:
        copy.wait_send()

    @pl.loop(0, NH)
    def _(i):
        halo_copy(i).wait_send()
        return_copy(i).wait_send()

    @pl.loop(0, NP)
    def _(block):
        given(dq_parts(block))
        given(dkv_parts(block))

    for away, stay in out_copies:
        away.wait()
        stay.wait()

    for dz in range(1, NZ):
        slot = (z + dz) % NZ
        pltpu.make_async_copy(ar_b.at[slot], ar_b.at[slot], arb_recv.at[slot]).wait()
    gains = jnp.sum(ar_b[...], axis=0)
    qterm_out[...] = gains[0:1]
    kterm_out[...] = gains[1:2]


def deliver(*refs):
    n = (len(refs) - 1) // 2
    copies = [pltpu.make_async_copy(refs[i], refs[n + i], refs[-1].at[i]) for i in range(n)]
    for copy in copies:
        copy.start()
    for copy in copies:
        copy.wait()


def per_device(query_input, key_input, saved_value_input, grad_output, query_gain, key_gain):
    frequency = (10000.0 ** (-np.arange(64, dtype=np.float64) / 64)).astype(np.float32)
    frequency = jnp.asarray(np.concatenate([frequency, frequency])[None, :])
    vmem = pl.BlockSpec(memory_space=pltpu.VMEM)
    dma = pltpu.SemaphoreType.DMA
    regular = pltpu.SemaphoreType.REGULAR
    span = (NP + NH) * T
    held = pl.BlockSpec(memory_space=pltpu.HBM)
    shapes = (
        jax.ShapeDtypeStruct((T, 16 * D), BF16),
        jax.ShapeDtypeStruct((T, 8 * D), BF16),
        jax.ShapeDtypeStruct((T, 8 * D), BF16),
        jax.ShapeDtypeStruct((1, D), F32),
        jax.ShapeDtypeStruct((1, D), F32),
    )
    results = pl.pallas_call(
        kernel,
        out_shape=shapes,
        in_specs=[held] * 7,
        out_specs=(vmem,) * 5,
        scratch_shapes=[
            pltpu.VMEM((1, D), F32),
            pltpu.VMEM((1, D), F32),
            pltpu.VMEM((1, D), F32),
            pltpu.VMEM((2, T, 4 * D), BF16),
            pltpu.VMEM((2, T, 8 * D), BF16),
            pltpu.VMEM((2, span, D), BF16),
            pltpu.VMEM((2, NP * T, 2 * D), BF16),
            pltpu.VMEM((span, D), BF16),
            pltpu.VMEM((NP + NH, D, T), BF16),
            pltpu.VMEM((span, D), F32),
            pltpu.VMEM((span, D), F32),
            pltpu.VMEM((NH + 1, T, 2 * T), F32),
            pltpu.VMEM((NH + 1, T, 2 * T), F32),
            pltpu.VMEM((2, span, D), F32),
            pltpu.VMEM((NP, T, 2 * D), BF16),
            pltpu.VMEM((NP, 2, T, D), BF16),
            pltpu.VMEM((NH, 2, T, D), BF16),
            pltpu.VMEM((NH, 2, T, D), BF16),
            pltpu.VMEM((2, T, 8 * D), BF16),
            pltpu.VMEM((2, 2, T, 4 * D), BF16),
            pltpu.VMEM((8, D), F32),
            pltpu.VMEM((NP, 8, D), F32),
            pltpu.VMEM((NZ, 8, D), F32),
            pltpu.VMEM((NX, 8, D), F32),
            dma((4,)),
            dma((4,)),
            dma((2, 2, 4)),
            dma((2, NP)),
            dma((2, 2, 4)),
            dma((2, NP)),
            dma((NH,)),
            dma((NH,)),
            dma((NH,)),
            dma((NH,)),
            dma((NP,)),
            dma((4, 2)),
            dma((NP,)),
            dma((4, 2)),
            dma((3,)),
            dma((3,)),
            dma((3,)),
            dma((NP,)),
            dma((NP,)),
            dma((NZ,)),
            dma((NZ,)),
            dma((NX,)),
            dma((NX,)),
            dma((3,)),
            regular,
            regular,
            regular,
            regular,
        ],
        compiler_params=pltpu.CompilerParams(
            collective_id=0, has_side_effects=True, vmem_limit_bytes=61 * 2**20
        ),
        cost_estimate=pl.CostEstimate(flops=1700000000, bytes_accessed=3000000, transcendentals=1400000),
    )(
        query_input,
        key_input,
        saved_value_input,
        grad_output,
        query_gain.reshape(1, D),
        key_gain.reshape(1, D),
        frequency,
    )
    dq, dk, dv, qterm, kterm = pl.pallas_call(
        deliver,
        out_shape=shapes,
        in_specs=[vmem] * 5,
        out_specs=(held,) * 5,
        scratch_shapes=[dma((5,))],
    )(*results)
    return dq, dk, dv, qterm.reshape(D), kterm.reshape(D)


def solution(mesh):
    tokens = P(("seq", "sub"), None)
    return jax.shard_map(
        per_device,
        mesh=mesh,
        in_specs=(tokens, tokens, tokens, tokens, P(), P()),
        out_specs=(tokens, tokens, tokens, P(), P()),
        check_vma=False,
    )
```

```python
import functools

import jax
import jax.numpy as jnp
import numpy as np
from jax import lax
from jax.experimental import pallas as pl
from jax.experimental.pallas import tpu as pltpu
from jax.sharding import PartitionSpec as P

MESH = pl.DeviceIdType.MESH
T = 128
D = 128
NP = 8
NH = 4
NZ = 16
NX = 4
EPS = 1e-6
SCALE = 168.0 ** (-0.5)
LOG2E = 1.4426950408889634
LN2 = 0.6931471805599453
F32 = jnp.float32
BF16 = jnp.bfloat16


def device(col, y, c):
    return ((col * 2 + y // 2) * 2 + c, y % 2)


def place(y, c):
    return 4 * (y // 2) + 2 * c + y % 2


def rows_of(block, blocks=1):
    return pl.ds(pl.multiple_of(block * T, T), blocks * T)


def cols_of(start, size):
    return pl.ds(pl.multiple_of(start, 128), size)


def unit_of(raw):
    inverse = lax.rsqrt(jnp.mean(raw * raw, axis=-1, keepdims=True) + EPS)
    return raw * inverse, inverse


def rope(rows, cosine, sine):
    return rows * cosine + pltpu.roll(rows, 64, 1) * sine


def rope_back(rows, cosine, sine):
    return rows * cosine - pltpu.roll(rows, 64, 1) * sine


def dot_nt(a, b):
    return lax.dot_general(a, b, (((1,), (1,)), ((), ())), preferred_element_type=F32)


def dot_nn(a, b):
    return jnp.dot(a, b, preferred_element_type=F32)


def kernel(
    q_in,
    k_in,
    v_in,
    g_in,
    qgain_in,
    kgain_in,
    freq_in,
    dq_out,
    dk_out,
    dv_out,
    qterm_out,
    kterm_out,
    qgain_ref,
    kgain_ref,
    freq_ref,
    st_kv,
    st_qg,
    kv,
    qg,
    kready,
    ktrans,
    ctab,
    stab,
    weights,
    gprobs,
    probs_low,
    grad_scores,
    dkv,
    dq_res,
    dkv_res,
    halo_res,
    halo_ret,
    plane_q,
    plane_kv,
    terms,
    ar_a,
    ar_b,
    ar_c,
    core_send,
    core_recv,
    kv_send,
    kv_recv,
    qg_send,
    qg_recv,
    halo_send,
    halo_recv,
    ret_send,
    ret_recv,
    dq_send,
    dq_recv,
    dkv_send,
    dkv_recv,
    out_send,
    out_recv,
    out_local,
    ara_send,
    ara_recv,
    arb_send,
    arb_recv,
    arc_send,
    arc_recv,
    small_sem,
    relay_up,
    relay_one,
    relay_two,
    relay_four,
):
    s = lax.axis_index("seq")
    c = s % 2
    col = s // 4
    y = 2 * ((s // 2) % 2) + lax.axis_index("sub")
    z = col % NZ
    x = col // NZ
    other = 1 - c
    mine = place(y, c)
    theirs = place(y, other)
    partner = device(col, y, other)
    after = device((col + 1) % (NX * NZ), y, c)
    before = device((col + NX * NZ - 1) % (NX * NZ), y, c)

    column_peers = [(dy, dc) for dy in range(4) for dc in range(2) if (dy, dc) != (0, 0)]

    def column_device(dy, dc):
        return device(col, (y + dy) % 4, (c + dc) % 2)

    def z_device(dz):
        return device(x * NZ + (z + dz) % NZ, y, c)

    def x_device(dx):
        return device(((x + dx) % NX) * NZ + z, y, c)

    def greet(semaphore, target):
        pl.semaphore_signal(semaphore, inc=1, device_id=target, device_id_type=MESH)

    def load_small(i):
        src, dst = ((qgain_in, qgain_ref), (kgain_in, kgain_ref), (freq_in, freq_ref))[i]
        return pltpu.make_async_copy(src, dst, small_sem.at[i])

    for i in range(3):
        load_small(i).start()

    barrier = pltpu.get_barrier_semaphore()
    greeted = [column_device(dy, dc) for dy, dc in column_peers]
    greeted += [before, z_device(NZ - 1), x_device(NX - 1)]
    for target in greeted:
        greet(barrier, target)
    pl.semaphore_wait(barrier, len(greeted))
    greet(relay_up, z_device(1))
    greet(relay_up, x_device(1))

    def remote(src, dst, send, recv, target):
        return pltpu.make_async_remote_copy(
            src_ref=src, dst_ref=dst, send_sem=send, recv_sem=recv, device_id=target, device_id_type=MESH
        )

    sends = []

    core_copies = []
    for i, (ref, width) in enumerate(((k_in, 4 * D), (v_in, 4 * D), (q_in, 8 * D), (g_in, 8 * D))):
        stage = st_kv.at[i] if i < 2 else st_qg.at[i - 2]
        core_copies.append(
            remote(ref.at[:, cols_of(other * width, width)], stage, core_send.at[i], core_recv.at[i], partner)
        )

    def spread(kind, sources, width, slots, first_row_block, send, recv, block, turn):
        for i, source in enumerate(sources):
            base, ref = source
            for dy in range(1, 4):
                yy = (y + dy) % 4
                copy = remote(
                    ref.at[:, cols_of(base + yy * width, width)],
                    slots.at[i, rows_of(first_row_block + block)],
                    send.at[turn, i, dy],
                    recv.at[i, block],
                    device(col, yy, c),
                )
                copy.start()
                sends.append(copy)
            pltpu.make_async_copy(
                ref.at[:, cols_of(base + y * width, width)],
                slots.at[i, rows_of(first_row_block + block)],
                recv.at[i, block],
            ).start()

    core_copies[0].start()
    core_copies[1].start()
    own_kv = [(c * 4 * D, k_in), (c * 4 * D, v_in)]
    spread("kv", own_kv, D, kv, NH, kv_send, kv_recv, mine, 0)
    core_copies[2].start()
    core_copies[3].start()
    core_copies[0].wait_recv()
    core_copies[1].wait_recv()
    spread("kv", [(0, st_kv.at[0]), (0, st_kv.at[1])], D, kv, NH, kv_send, kv_recv, theirs, 1)
    own_qg = [(c * 8 * D, q_in), (c * 8 * D, g_in)]
    spread("qg", own_qg, 2 * D, qg, 0, qg_send, qg_recv, mine, 0)
    core_copies[2].wait_recv()
    core_copies[3].wait_recv()
    spread("qg", [(0, st_qg.at[0]), (0, st_qg.at[1])], 2 * D, qg, 0, qg_send, qg_recv, theirs, 1)

    for i in range(3):
        load_small(i).wait()

    first_token = col * (NP * T) - NH * T
    half = (NP + NH) * T // 2
    step_rows = 64

    @pl.loop(0, half // step_rows)
    def _(step):
        row = lax.broadcasted_iota(jnp.int32, (step_rows, D), 0)
        lane = lax.broadcasted_iota(jnp.int32, (step_rows, D), 1)
        low = lane < 64
        token = first_token + step * step_rows + row + jnp.where(low, 0, half)
        angle = token.astype(F32) * freq_ref[...]
        cosine = jnp.cos(angle)
        sine = jnp.sin(angle)
        cosine_turned = pltpu.roll(cosine, 64, 1)
        sine_turned = pltpu.roll(sine, 64, 1)
        near = pl.ds(pl.multiple_of(step * step_rows, step_rows), step_rows)
        far = pl.ds(pl.multiple_of(half + step * step_rows, step_rows), step_rows)
        ctab[near] = jnp.where(low, cosine, cosine_turned)
        ctab[far] = jnp.where(low, cosine_turned, cosine)
        stab[near] = jnp.where(low, -sine, sine_turned)
        stab[far] = jnp.where(low, -sine_turned, sine)

    dkv[...] = jnp.zeros_like(dkv)
    terms[...] = jnp.zeros_like(terms)
    kgain = kgain_ref[...]
    qgain = qgain_ref[...]

    def wait_kv(block):
        for i in range(2):
            slot = kv.at[i, rows_of(NH + block)]
            pltpu.make_async_copy(slot, slot, kv_recv.at[i, block]).wait()

    def halo_copy(i):
        return remote(
            kv.at[:, rows_of(NP + i)], kv.at[:, rows_of(i)], halo_send.at[i], halo_recv.at[i], after
        )

    def prepare_keys(block):
        rows = rows_of(block, NH)
        unit, _ = unit_of(kv[0, rows].astype(F32))
        turned = rope(unit * kgain, ctab[rows], stab[rows])
        kready[rows] = turned.astype(BF16)
        ktrans[:, cols_of(block * T, NH * T)] = turned.T.astype(BF16)

    @pl.loop(0, NH)
    def _(turn):
        core = turn // 2 + c - 2 * (turn // 2) * c
        i = 2 * core + turn % 2
        wait_kv(NH + i)
        halo_copy(i).start()

    pl.semaphore_wait(relay_up, 2)
    for target in (z_device(1), z_device(NZ - 1), x_device(1), x_device(NX - 1)):
        greet(relay_one, target)

    @pl.loop(0, NH)
    def _(i):
        wait_kv(i)

    prepare_keys(NH)
    prepare_keys(2 * NH)

    pl.semaphore_wait(relay_one, 4)
    greet(relay_two, z_device(2))
    greet(relay_two, z_device(NZ - 2))

    halo_valid = jnp.where(col == 0, 0.0, 1.0)
    key_row = lax.broadcasted_iota(jnp.int32, (T, 2 * T), 0)
    query_lane = lax.broadcasted_iota(jnp.int32, (T, 2 * T), 1) % T
    newer = key_row > query_lane

    def norm_back(turned_grad, raw, gain, cosine, sine):
        unit, inverse = unit_of(raw)
        w = rope_back(turned_grad, cosine, sine)
        term = jnp.sum(w * unit, axis=0, keepdims=True)
        grad_unit = w * gain
        grad = (grad_unit - unit * jnp.mean(grad_unit * unit, axis=-1, keepdims=True)) * inverse
        return grad.astype(BF16), term

    def owner(block):
        return 2 * (block // 4) + block % 2, (block // 2) % 2

    def dq_parts(block):
        yy, cc = owner(block)
        return dq_res.at[block], plane_q.at[cc, :, cols_of(y * 2 * D, 2 * D)], dq_send.at[block], dq_recv.at[y, cc], yy

    def dkv_parts(block):
        yy, cc = owner(block)
        return dkv_res.at[block], plane_kv.at[cc, :, :, cols_of(y * D, D)], dkv_send.at[block], dkv_recv.at[y, cc], yy

    def give(parts):
        src, dst, send, recv, yy = parts

        @pl.when(yy == y)
        def _():
            pltpu.make_async_copy(src, dst, recv).start()

        @pl.when(yy != y)
        def _():
            remote(src, dst, send, recv, device(col, yy, c)).start()

    def given(parts):
        src, dst, send, recv, yy = parts

        @pl.when(yy != y)
        def _():
            remote(src, dst, send, recv, device(col, yy, c)).wait_send()

    def attend(block):
        rows = rows_of(block)
        for i in range(2):
            slot = qg.at[i, rows]
            pltpu.make_async_copy(slot, slot, qg_recv.at[i, block]).wait()
        own = rows_of(block + NH)
        cosine, sine = ctab[own], stab[own]
        raw = [qg[0, rows, h * D : (h + 1) * D].astype(F32) for h in range(2)]
        queries = jnp.concatenate(
            [(rope(unit_of(r)[0] * qgain, cosine, sine) * (SCALE * LOG2E)).astype(BF16) for r in raw], axis=0
        )
        grads = jnp.concatenate([qg[1, rows, h * D : (h + 1) * D] for h in range(2)], axis=0)
        window = pl.ds(pl.multiple_of(block * T, T), (NH + 1) * T)
        weights[...] = dot_nt(kready[window], queries)
        gprobs[...] = dot_nt(kv[1, window], grads)
        total = jnp.zeros((1, 2 * T), F32)
        inner = jnp.zeros((1, 2 * T), F32)
        for t in range(NH + 1):
            part = slice(t * T, (t + 1) * T)
            weight = jnp.exp2(weights[part])
            if t == 0:
                weight = jnp.where(newer, weight, 0.0)
            if t == NH:
                weight = jnp.where(newer, 0.0, weight)
            else:
                weight = weight * jnp.where(block + t < NH, halo_valid, 1.0)
            total = total + jnp.sum(weight, axis=0, keepdims=True)
            inner = inner + jnp.sum(weight * gprobs[part], axis=0, keepdims=True)
            weights[part] = weight
        inverse = 1.0 / total
        inner = inner * inverse
        for t in range(NH + 1):
            part = slice(t * T, (t + 1) * T)
            prob = weights[part] * inverse
            probs_low[part] = prob.astype(BF16)
            grad_scores[part] = (prob * (gprobs[part] - inner)).astype(BF16)
        dkv[1, window] += dot_nn(probs_low[...], grads)
        dkv[0, window] += dot_nn(grad_scores[...], queries)
        grad_query = dot_nn(ktrans[:, cols_of(block * T, (NH + 1) * T)], grad_scores[...])
        for h in range(2):
            turned = grad_query[:, h * T : (h + 1) * T].T * SCALE
            grad, term = norm_back(turned, raw[h], qgain, cosine, sine)
            dq_res[block, :, h * D : (h + 1) * D] = grad
            terms[0:1] += term

    late = jnp.where(z == 0, 1, 0)
    halo_turn = 2 + 2 * late

    @pl.loop(0, NP)
    def _(i):
        @pl.when(i == halo_turn)
        def _():
            @pl.loop(0, NH)
            def _(j):
                halo_copy(j).wait_recv()

            prepare_keys(0)

            pl.semaphore_wait(relay_two, 2)
            greet(relay_four, z_device(4))
            greet(relay_four, z_device(NZ - 4))

        major, minor = i // 4, (i // 2) % 2
        first = late * major + (1 - late) * minor
        swapped = late * minor + (1 - late) * major
        core = swapped + c - 2 * swapped * c
        attend(4 * (1 - first) + 2 * core + i % 2)

    def return_copy(i):
        return remote(halo_res.at[i], halo_ret.at[i], ret_send.at[i], ret_recv.at[i], before)

    @pl.loop(0, NH)
    def _(block):
        keys = rows_of(block)
        halo_res[block, 0] = (dkv[0, keys] * LN2).astype(BF16)
        halo_res[block, 1] = dkv[1, keys].astype(BF16)
        return_copy(block).start()

    @pl.loop(0, (NH + NP) // NH)
    def _(part):
        keys = rows_of(part * NH, NH)
        unit, _ = unit_of(kv[0, keys].astype(F32))
        w = rope_back(dkv[0, keys] * LN2, ctab[keys], stab[keys])
        terms[1:2] += jnp.sum(w * unit, axis=0, keepdims=True)

    ar_a[mine] = terms[...]
    stage_a = [
        remote(terms, ar_a.at[mine], ara_send.at[i], ara_recv.at[mine], column_device(dy, dc))
        for i, (dy, dc) in enumerate(column_peers)
    ]
    for copy in stage_a:
        copy.start()

    @pl.loop(0, NP)
    def _(block):
        give(dq_parts(block))
    for dy, dc in column_peers:
        slot = place((y + dy) % 4, (c + dc) % 2)
        pltpu.make_async_copy(ar_a.at[slot], ar_a.at[slot], ara_recv.at[slot]).wait()
    ar_c[x] = jnp.sum(ar_a[...], axis=0)
    stage_c = [
        remote(ar_c.at[x], ar_c.at[x], arc_send.at[dx], arc_recv.at[x], x_device(dx)) for dx in range(1, NX)
    ]
    for copy in stage_c:
        copy.start()


    keys = rows_of(NH, NH)
    grad, _ = norm_back(dkv[0, keys] * LN2, kv[0, keys].astype(F32), kgain, ctab[keys], stab[keys])
    dkv_res[0:NH, 0] = grad.reshape(NH, T, D)
    dkv_res[0:NH, 1] = dkv[1, keys].astype(BF16).reshape(NH, T, D)

    @pl.loop(0, NH)
    def _(block):
        give(dkv_parts(block))

    pl.semaphore_wait(relay_four, 2)
    for dx in range(1, NX):
        slot = (x + dx) % NX
        pltpu.make_async_copy(ar_c.at[slot], ar_c.at[slot], arc_recv.at[slot]).wait()
    ar_b[z] = jnp.sum(ar_c[...], axis=0)
    farthest_first = sorted(range(1, NZ), key=lambda dz: abs(dz - NZ // 2))
    stage_b = [
        remote(ar_b.at[z], ar_b.at[z], arb_send.at[dz], arb_recv.at[z], z_device(dz)) for dz in farthest_first
    ]
    for copy in stage_b:
        copy.start()

    @pl.loop(NH, NP)
    def _(block):
        return_copy(block - NH).wait_recv()
        keys = rows_of(block + NH)
        grad_key = dkv[0, keys] * LN2 + halo_ret[block - NH, 0].astype(F32)
        grad, _ = norm_back(grad_key, kv[0, keys].astype(F32), kgain, ctab[keys], stab[keys])
        dkv_res[block, 0] = grad
        dkv_res[block, 1] = (dkv[1, keys] + halo_ret[block - NH, 1].astype(F32)).astype(BF16)
        give(dkv_parts(block))

    wide, narrow = cols_of(c * 8 * D, 8 * D), cols_of(c * 4 * D, 4 * D)
    plane_parts = (
        (lambda cc: plane_q.at[cc], dq_out.at[:, wide]),
        (lambda cc: plane_kv.at[cc, 0], dk_out.at[:, narrow]),
        (lambda cc: plane_kv.at[cc, 1], dv_out.at[:, narrow]),
    )
    out_copies = []
    for i, (part, target) in enumerate(plane_parts):
        if i < 2:
            for cc in range(2):
                for yy in range(4):
                    if i == 0:
                        slot = plane_q.at[cc, :, cols_of(yy * 2 * D, 2 * D)]
                        sem = dq_recv.at[yy, cc]
                    else:
                        slot = plane_kv.at[cc, :, :, cols_of(yy * D, D)]
                        sem = dkv_recv.at[yy, cc]
                    pltpu.make_async_copy(slot, slot, sem).wait()
        away = remote(part(other), target, out_send.at[i], out_recv.at[i], partner)
        stay = pltpu.make_async_copy(part(c), target, out_local.at[i])
        away.start()
        stay.start()
        out_copies.append((away, stay))

    for copy in core_copies + sends + stage_a + stage_b + stage_c:
        copy.wait_send()

    @pl.loop(0, NH)
    def _(i):
        halo_copy(i).wait_send()
        return_copy(i).wait_send()

    @pl.loop(0, NP)
    def _(block):
        given(dq_parts(block))
        given(dkv_parts(block))

    for away, stay in out_copies:
        away.wait()
        stay.wait()

    for dz in range(1, NZ):
        slot = (z + dz) % NZ
        pltpu.make_async_copy(ar_b.at[slot], ar_b.at[slot], arb_recv.at[slot]).wait()
    gains = jnp.sum(ar_b[...], axis=0)
    qterm_out[...] = gains[0:1]
    kterm_out[...] = gains[1:2]


def deliver(*refs):
    n = (len(refs) - 1) // 2
    copies = [pltpu.make_async_copy(refs[i], refs[n + i], refs[-1].at[i]) for i in range(n)]
    for copy in copies:
        copy.start()
    for copy in copies:
        copy.wait()


def per_device(query_input, key_input, saved_value_input, grad_output, query_gain, key_gain):
    frequency = (10000.0 ** (-np.arange(64, dtype=np.float64) / 64)).astype(np.float32)
    frequency = jnp.asarray(np.concatenate([frequency, frequency])[None, :])
    vmem = pl.BlockSpec(memory_space=pltpu.VMEM)
    dma = pltpu.SemaphoreType.DMA
    regular = pltpu.SemaphoreType.REGULAR
    span = (NP + NH) * T
    held = pl.BlockSpec(memory_space=pltpu.HBM)
    shapes = (
        jax.ShapeDtypeStruct((T, 16 * D), BF16),
        jax.ShapeDtypeStruct((T, 8 * D), BF16),
        jax.ShapeDtypeStruct((T, 8 * D), BF16),
        jax.ShapeDtypeStruct((1, D), F32),
        jax.ShapeDtypeStruct((1, D), F32),
    )
    results = pl.pallas_call(
        kernel,
        out_shape=tuple(pltpu.VMEM(sh.shape, sh.dtype) for sh in shapes),
        in_specs=[held] * 7,
        out_specs=(vmem,) * 5,
        scratch_shapes=[
            pltpu.VMEM((1, D), F32),
            pltpu.VMEM((1, D), F32),
            pltpu.VMEM((1, D), F32),
            pltpu.VMEM((2, T, 4 * D), BF16),
            pltpu.VMEM((2, T, 8 * D), BF16),
            pltpu.VMEM((2, span, D), BF16),
            pltpu.VMEM((2, NP * T, 2 * D), BF16),
            pltpu.VMEM((span, D), BF16),
            pltpu.VMEM((D, span), BF16),
            pltpu.VMEM((span, D), F32),
            pltpu.VMEM((span, D), F32),
            pltpu.VMEM(((NH + 1) * T, 2 * T), F32),
            pltpu.VMEM(((NH + 1) * T, 2 * T), F32),
            pltpu.VMEM(((NH + 1) * T, 2 * T), BF16),
            pltpu.VMEM(((NH + 1) * T, 2 * T), BF16),
            pltpu.VMEM((2, span, D), F32),
            pltpu.VMEM((NP, T, 2 * D), BF16),
            pltpu.VMEM((NP, 2, T, D), BF16),
            pltpu.VMEM((NH, 2, T, D), BF16),
            pltpu.VMEM((NH, 2, T, D), BF16),
            pltpu.VMEM((2, T, 8 * D), BF16),
            pltpu.VMEM((2, 2, T, 4 * D), BF16),
            pltpu.VMEM((8, D), F32),
            pltpu.VMEM((NP, 8, D), F32),
            pltpu.VMEM((NZ, 8, D), F32),
            pltpu.VMEM((NX, 8, D), F32),
            dma((4,)),
            dma((4,)),
            dma((2, 2, 4)),
            dma((2, NP)),
            dma((2, 2, 4)),
            dma((2, NP)),
            dma((NH,)),
            dma((NH,)),
            dma((NH,)),
            dma((NH,)),
            dma((NP,)),
            dma((4, 2)),
            dma((NP,)),
            dma((4, 2)),
            dma((3,)),
            dma((3,)),
            dma((3,)),
            dma((NP,)),
            dma((NP,)),
            dma((NZ,)),
            dma((NZ,)),
            dma((NX,)),
            dma((NX,)),
            dma((3,)),
            regular,
            regular,
            regular,
            regular,
        ],
        compiler_params=pltpu.CompilerParams(
            collective_id=0, has_side_effects=True, vmem_limit_bytes=61 * 2**20
        ),
        cost_estimate=pl.CostEstimate(flops=1700000000, bytes_accessed=3000000, transcendentals=1400000),
    )(
        query_input,
        key_input,
        saved_value_input,
        grad_output,
        query_gain.reshape(1, D),
        key_gain.reshape(1, D),
        frequency,
    )
    dq, dk, dv, qterm, kterm = pl.pallas_call(
        deliver,
        out_shape=shapes,
        in_specs=[pl.BlockSpec(memory_space=pl.ANY)] * 5,
        out_specs=(held,) * 5,
        scratch_shapes=[dma((5,))],
        compiler_params=pltpu.CompilerParams(vmem_limit_bytes=2**20),
    )(*results)
    return dq, dk, dv, qterm.reshape(D), kterm.reshape(D)


def solution(mesh):
    tokens = P(("seq", "sub"), None)
    return jax.shard_map(
        per_device,
        mesh=mesh,
        in_specs=(tokens, tokens, tokens, tokens, P(), P()),
        out_specs=(tokens, tokens, tokens, P(), P()),
        check_vma=False,
    )
```

```python
import functools

import jax
import jax.numpy as jnp
import numpy as np
from jax import lax
from jax.experimental import pallas as pl
from jax.experimental.pallas import tpu as pltpu
from jax.sharding import PartitionSpec as P

MESH = pl.DeviceIdType.MESH
T = 128
D = 128
NP = 8
NH = 4
NZ = 16
NX = 4
EPS = 1e-6
SCALE = 168.0 ** (-0.5)
LOG2E = 1.4426950408889634
LN2 = 0.6931471805599453
F32 = jnp.float32
BF16 = jnp.bfloat16


def device(col, y, c):
    return ((col * 2 + y // 2) * 2 + c, y % 2)


def place(y, c):
    return 4 * (y // 2) + 2 * c + y % 2


def rows_of(block, blocks=1):
    return pl.ds(pl.multiple_of(block * T, T), blocks * T)


def cols_of(start, size):
    return pl.ds(pl.multiple_of(start, 128), size)


def unit_of(raw):
    inverse = lax.rsqrt(jnp.mean(raw * raw, axis=-1, keepdims=True) + EPS)
    return raw * inverse, inverse


def rope(rows, cosine, sine):
    return rows * cosine + pltpu.roll(rows, 64, 1) * sine


def rope_back(rows, cosine, sine):
    return rows * cosine - pltpu.roll(rows, 64, 1) * sine


def dot_nt(a, b):
    return lax.dot_general(a, b, (((1,), (1,)), ((), ())), preferred_element_type=F32)


def dot_nn(a, b):
    return jnp.dot(a, b, preferred_element_type=F32)


def kernel(
    q_in,
    k_in,
    v_in,
    g_in,
    qgain_in,
    kgain_in,
    freq_in,
    dq_out,
    dk_out,
    dv_out,
    qterm_out,
    kterm_out,
    qgain_ref,
    kgain_ref,
    freq_ref,
    st_kv,
    st_qg,
    kv,
    qg,
    kready,
    kunit,
    ktrans,
    ctab,
    stab,
    weights,
    gprobs,
    probs_low,
    grad_scores,
    dkv,
    dq_res,
    dkv_res,
    halo_res,
    halo_ret,
    plane_q,
    plane_kv,
    terms,
    ar_a,
    ar_b,
    ar_c,
    core_send,
    core_recv,
    kv_send,
    kv_recv,
    qg_send,
    qg_recv,
    halo_send,
    halo_recv,
    ret_send,
    ret_recv,
    dq_send,
    dq_recv,
    dkv_send,
    dkv_recv,
    out_send,
    out_recv,
    out_local,
    ara_send,
    ara_recv,
    arb_send,
    arb_recv,
    arc_send,
    arc_recv,
    small_sem,
    relay_up,
    relay_one,
    relay_two,
    relay_four,
):
    s = lax.axis_index("seq")
    c = s % 2
    col = s // 4
    y = 2 * ((s // 2) % 2) + lax.axis_index("sub")
    z = col % NZ
    x = col // NZ
    other = 1 - c
    mine = place(y, c)
    theirs = place(y, other)
    partner = device(col, y, other)
    after = device((col + 1) % (NX * NZ), y, c)
    before = device((col + NX * NZ - 1) % (NX * NZ), y, c)

    column_peers = [(dy, dc) for dy in range(4) for dc in range(2) if (dy, dc) != (0, 0)]

    def column_device(dy, dc):
        return device(col, (y + dy) % 4, (c + dc) % 2)

    def z_device(dz):
        return device(x * NZ + (z + dz) % NZ, y, c)

    def x_device(dx):
        return device(((x + dx) % NX) * NZ + z, y, c)

    def greet(semaphore, target):
        pl.semaphore_signal(semaphore, inc=1, device_id=target, device_id_type=MESH)

    def load_small(i):
        src, dst = ((qgain_in, qgain_ref), (kgain_in, kgain_ref), (freq_in, freq_ref))[i]
        return pltpu.make_async_copy(src, dst, small_sem.at[i])

    for i in range(3):
        load_small(i).start()

    barrier = pltpu.get_barrier_semaphore()
    greeted = [column_device(dy, dc) for dy, dc in column_peers]
    greeted += [before, z_device(NZ - 1), x_device(NX - 1)]
    for target in greeted:
        greet(barrier, target)
    pl.semaphore_wait(barrier, len(greeted))
    greet(relay_up, z_device(1))
    greet(relay_up, x_device(1))

    def remote(src, dst, send, recv, target):
        return pltpu.make_async_remote_copy(
            src_ref=src, dst_ref=dst, send_sem=send, recv_sem=recv, device_id=target, device_id_type=MESH
        )

    sends = []

    core_copies = []
    for i, (ref, width) in enumerate(((k_in, 4 * D), (v_in, 4 * D), (q_in, 8 * D), (g_in, 8 * D))):
        stage = st_kv.at[i] if i < 2 else st_qg.at[i - 2]
        core_copies.append(
            remote(ref.at[:, cols_of(other * width, width)], stage, core_send.at[i], core_recv.at[i], partner)
        )

    def spread(kind, sources, width, slots, first_row_block, send, recv, block, turn):
        for i, source in enumerate(sources):
            base, ref = source
            for dy in range(1, 4):
                yy = (y + dy) % 4
                copy = remote(
                    ref.at[:, cols_of(base + yy * width, width)],
                    slots.at[i, rows_of(first_row_block + block)],
                    send.at[turn, i, dy],
                    recv.at[i, block],
                    device(col, yy, c),
                )
                copy.start()
                sends.append(copy)
            pltpu.make_async_copy(
                ref.at[:, cols_of(base + y * width, width)],
                slots.at[i, rows_of(first_row_block + block)],
                recv.at[i, block],
            ).start()

    core_copies[0].start()
    core_copies[1].start()
    own_kv = [(c * 4 * D, k_in), (c * 4 * D, v_in)]
    spread("kv", own_kv, D, kv, NH, kv_send, kv_recv, mine, 0)
    core_copies[2].start()
    core_copies[3].start()
    core_copies[0].wait_recv()
    core_copies[1].wait_recv()
    spread("kv", [(0, st_kv.at[0]), (0, st_kv.at[1])], D, kv, NH, kv_send, kv_recv, theirs, 1)
    own_qg = [(c * 8 * D, q_in), (c * 8 * D, g_in)]
    spread("qg", own_qg, 2 * D, qg, 0, qg_send, qg_recv, mine, 0)
    core_copies[2].wait_recv()
    core_copies[3].wait_recv()
    spread("qg", [(0, st_qg.at[0]), (0, st_qg.at[1])], 2 * D, qg, 0, qg_send, qg_recv, theirs, 1)

    for i in range(3):
        load_small(i).wait()

    first_token = col * (NP * T) - NH * T
    half = (NP + NH) * T // 2
    step_rows = 64

    @pl.loop(0, half // step_rows)
    def _(step):
        row = lax.broadcasted_iota(jnp.int32, (step_rows, D), 0)
        lane = lax.broadcasted_iota(jnp.int32, (step_rows, D), 1)
        low = lane < 64
        token = first_token + step * step_rows + row + jnp.where(low, 0, half)
        angle = token.astype(F32) * freq_ref[...]
        cosine = jnp.cos(angle)
        sine = jnp.sin(angle)
        cosine_turned = pltpu.roll(cosine, 64, 1)
        sine_turned = pltpu.roll(sine, 64, 1)
        near = pl.ds(pl.multiple_of(step * step_rows, step_rows), step_rows)
        far = pl.ds(pl.multiple_of(half + step * step_rows, step_rows), step_rows)
        ctab[near] = jnp.where(low, cosine, cosine_turned)
        ctab[far] = jnp.where(low, cosine_turned, cosine)
        stab[near] = jnp.where(low, -sine, sine_turned)
        stab[far] = jnp.where(low, -sine_turned, sine)

    dkv[...] = jnp.zeros_like(dkv)
    terms[...] = jnp.zeros_like(terms)
    kgain = kgain_ref[...]
    qgain = qgain_ref[...]

    def wait_kv(block):
        for i in range(2):
            slot = kv.at[i, rows_of(NH + block)]
            pltpu.make_async_copy(slot, slot, kv_recv.at[i, block]).wait()

    def halo_copy(i):
        return remote(
            kv.at[:, rows_of(NP + i)], kv.at[:, rows_of(i)], halo_send.at[i], halo_recv.at[i], after
        )

    def prepare_keys(block):
        rows = rows_of(block, NH)
        unit, _ = unit_of(kv[0, rows].astype(F32))
        turned = rope(unit * kgain, ctab[rows], stab[rows])
        kunit[rows] = unit
        kready[rows] = turned.astype(BF16)
        ktrans[:, cols_of(block * T, NH * T)] = turned.T.astype(BF16)

    @pl.loop(0, NH)
    def _(turn):
        core = turn // 2 + c - 2 * (turn // 2) * c
        i = 2 * core + turn % 2
        wait_kv(NH + i)
        halo_copy(i).start()

    pl.semaphore_wait(relay_up, 2)
    for target in (z_device(1), z_device(NZ - 1), x_device(1), x_device(NX - 1)):
        greet(relay_one, target)

    @pl.loop(0, NH)
    def _(i):
        wait_kv(i)

    prepare_keys(NH)
    prepare_keys(2 * NH)

    pl.semaphore_wait(relay_one, 4)
    greet(relay_two, z_device(2))
    greet(relay_two, z_device(NZ - 2))

    halo_valid = jnp.where(col == 0, 0.0, 1.0)
    key_row = lax.broadcasted_iota(jnp.int32, (T, 2 * T), 0)
    query_lane = lax.broadcasted_iota(jnp.int32, (T, 2 * T), 1) % T
    newer = key_row > query_lane

    def norm_back(turned_grad, raw, gain, cosine, sine):
        unit, inverse = unit_of(raw)
        w = rope_back(turned_grad, cosine, sine)
        term = jnp.sum(w * unit, axis=0, keepdims=True)
        grad_unit = w * gain
        grad = (grad_unit - unit * jnp.mean(grad_unit * unit, axis=-1, keepdims=True)) * inverse
        return grad.astype(BF16), term

    def owner(block):
        return 2 * (block // 4) + block % 2, (block // 2) % 2

    def dq_parts(block):
        yy, cc = owner(block)
        return dq_res.at[block], plane_q.at[cc, :, cols_of(y * 2 * D, 2 * D)], dq_send.at[block], dq_recv.at[y, cc], yy

    def dkv_parts(block):
        yy, cc = owner(block)
        return dkv_res.at[block], plane_kv.at[cc, :, :, cols_of(y * D, D)], dkv_send.at[block], dkv_recv.at[y, cc], yy

    def give(parts):
        src, dst, send, recv, yy = parts

        @pl.when(yy == y)
        def _():
            pltpu.make_async_copy(src, dst, recv).start()

        @pl.when(yy != y)
        def _():
            remote(src, dst, send, recv, device(col, yy, c)).start()

    def given(parts):
        src, dst, send, recv, yy = parts

        @pl.when(yy != y)
        def _():
            remote(src, dst, send, recv, device(col, yy, c)).wait_send()

    def attend(first_block):
        blocks = [first_block, first_block + 1]
        for block in blocks:
            for i in range(2):
                slot = qg.at[i, rows_of(block)]
                pltpu.make_async_copy(slot, slot, qg_recv.at[i, block]).wait()
        raws, queries, grads, turns = [], [], [], []
        for block in blocks:
            rows, own = rows_of(block), rows_of(block + NH)
            cosine, sine = ctab[own], stab[own]
            raw = [qg[0, rows, h * D : (h + 1) * D].astype(F32) for h in range(2)]
            turned = [(rope(unit_of(r)[0] * qgain, cosine, sine) * (SCALE * LOG2E)).astype(BF16) for r in raw]
            raws.append(raw)
            turns.append((cosine, sine))
            queries.append(jnp.concatenate(turned, axis=0))
            grads.append(jnp.concatenate([qg[1, rows, h * D : (h + 1) * D] for h in range(2)], axis=0))
        for n, block in enumerate(blocks):
            window = rows_of(block, NH + 1)
            weights[n] = dot_nt(kready[window], queries[n])
            gprobs[n] = dot_nt(kv[1, window], grads[n])
        sums = []
        for n, block in enumerate(blocks):
            total = jnp.zeros((1, 2 * T), F32)
            inner = jnp.zeros((1, 2 * T), F32)
            for t in range(NH + 1):
                part = slice(t * T, (t + 1) * T)
                weight = jnp.exp2(weights[n, part])
                if t == 0:
                    weight = jnp.where(newer, weight, 0.0)
                if t == NH:
                    weight = jnp.where(newer, 0.0, weight)
                else:
                    weight = weight * jnp.where(block + t < NH, halo_valid, 1.0)
                total = total + jnp.sum(weight, axis=0, keepdims=True)
                inner = inner + jnp.sum(weight * gprobs[n, part], axis=0, keepdims=True)
                weights[n, part] = weight
            inverse = 1.0 / total
            sums.append((inverse, inner * inverse))
        for n, block in enumerate(blocks):
            inverse, inner = sums[n]
            for t in range(NH + 1):
                part = slice(t * T, (t + 1) * T)
                prob = weights[n, part] * inverse
                probs_low[n, part] = prob.astype(BF16)
                grad_scores[n, part] = (prob * (gprobs[n, part] - inner)).astype(BF16)
        grad_query = [
            dot_nn(ktrans[:, cols_of(block * T, (NH + 1) * T)], grad_scores[n]) for n, block in enumerate(blocks)
        ]
        for n, block in enumerate(blocks):
            window = rows_of(block, NH + 1)
            dkv[1, window] += dot_nn(probs_low[n], grads[n])
            dkv[0, window] += dot_nn(grad_scores[n], queries[n])
        terms_here = jnp.zeros((1, D), F32)
        for n, block in enumerate(blocks):
            for h in range(2):
                turned = grad_query[n][:, h * T : (h + 1) * T].T * SCALE
                grad, term = norm_back(turned, raws[n][h], qgain, *turns[n])
                dq_res[block, :, h * D : (h + 1) * D] = grad
                terms_here = terms_here + term
        terms[0:1] += terms_here

    late = jnp.where(z == 0, 1, 0)
    halo_turn = 1 + late

    @pl.loop(0, NP // 2)
    def _(i):
        @pl.when(i == halo_turn)
        def _():
            @pl.loop(0, NH)
            def _(j):
                halo_copy(j).wait_recv()

            prepare_keys(0)

            pl.semaphore_wait(relay_two, 2)
            greet(relay_four, z_device(4))
            greet(relay_four, z_device(NZ - 4))

        major, minor = i // 2, i % 2
        first = late * major + (1 - late) * minor
        swapped = late * minor + (1 - late) * major
        core = swapped + c - 2 * swapped * c
        attend(4 * (1 - first) + 2 * core)

    def return_copy(i):
        return remote(halo_res.at[i], halo_ret.at[i], ret_send.at[i], ret_recv.at[i], before)

    @pl.loop(0, NH)
    def _(block):
        keys = rows_of(block)
        halo_res[block, 0] = (dkv[0, keys] * LN2).astype(BF16)
        halo_res[block, 1] = dkv[1, keys].astype(BF16)
        return_copy(block).start()

    @pl.loop(0, (NH + NP) // NH)
    def _(part):
        keys = rows_of(part * NH, NH)
        w = rope_back(dkv[0, keys] * LN2, ctab[keys], stab[keys])
        terms[1:2] += jnp.sum(w * kunit[keys], axis=0, keepdims=True)

    ar_a[mine] = terms[...]
    stage_a = [
        remote(terms, ar_a.at[mine], ara_send.at[i], ara_recv.at[mine], column_device(dy, dc))
        for i, (dy, dc) in enumerate(column_peers)
    ]
    for copy in stage_a:
        copy.start()

    @pl.loop(0, NP)
    def _(block):
        give(dq_parts(block))
    for dy, dc in column_peers:
        slot = place((y + dy) % 4, (c + dc) % 2)
        pltpu.make_async_copy(ar_a.at[slot], ar_a.at[slot], ara_recv.at[slot]).wait()
    ar_c[x] = jnp.sum(ar_a[...], axis=0)
    stage_c = [
        remote(ar_c.at[x], ar_c.at[x], arc_send.at[dx], arc_recv.at[x], x_device(dx)) for dx in range(1, NX)
    ]
    for copy in stage_c:
        copy.start()


    keys = rows_of(NH, NH)
    grad, _ = norm_back(dkv[0, keys] * LN2, kv[0, keys].astype(F32), kgain, ctab[keys], stab[keys])
    dkv_res[0:NH, 0] = grad.reshape(NH, T, D)
    dkv_res[0:NH, 1] = dkv[1, keys].astype(BF16).reshape(NH, T, D)

    @pl.loop(0, NH)
    def _(block):
        give(dkv_parts(block))

    pl.semaphore_wait(relay_four, 2)
    for dx in range(1, NX):
        slot = (x + dx) % NX
        pltpu.make_async_copy(ar_c.at[slot], ar_c.at[slot], arc_recv.at[slot]).wait()
    ar_b[z] = jnp.sum(ar_c[...], axis=0)
    farthest_first = sorted(range(1, NZ), key=lambda dz: abs(dz - NZ // 2))
    stage_b = [
        remote(ar_b.at[z], ar_b.at[z], arb_send.at[dz], arb_recv.at[z], z_device(dz)) for dz in farthest_first
    ]
    for copy in stage_b:
        copy.start()

    @pl.loop(NH, NP)
    def _(block):
        return_copy(block - NH).wait_recv()
        keys = rows_of(block + NH)
        grad_key = dkv[0, keys] * LN2 + halo_ret[block - NH, 0].astype(F32)
        grad, _ = norm_back(grad_key, kv[0, keys].astype(F32), kgain, ctab[keys], stab[keys])
        dkv_res[block, 0] = grad
        dkv_res[block, 1] = (dkv[1, keys] + halo_ret[block - NH, 1].astype(F32)).astype(BF16)
        give(dkv_parts(block))

    wide, narrow = cols_of(c * 8 * D, 8 * D), cols_of(c * 4 * D, 4 * D)
    plane_parts = (
        (lambda cc: plane_q.at[cc], dq_out.at[:, wide]),
        (lambda cc: plane_kv.at[cc, 0], dk_out.at[:, narrow]),
        (lambda cc: plane_kv.at[cc, 1], dv_out.at[:, narrow]),
    )
    out_copies = []
    for i, (part, target) in enumerate(plane_parts):
        if i < 2:
            for cc in range(2):
                for yy in range(4):
                    if i == 0:
                        slot = plane_q.at[cc, :, cols_of(yy * 2 * D, 2 * D)]
                        sem = dq_recv.at[yy, cc]
                    else:
                        slot = plane_kv.at[cc, :, :, cols_of(yy * D, D)]
                        sem = dkv_recv.at[yy, cc]
                    pltpu.make_async_copy(slot, slot, sem).wait()
        away = remote(part(other), target, out_send.at[i], out_recv.at[i], partner)
        stay = pltpu.make_async_copy(part(c), target, out_local.at[i])
        away.start()
        stay.start()
        out_copies.append((away, stay))

    for copy in core_copies + sends + stage_a + stage_b + stage_c:
        copy.wait_send()

    @pl.loop(0, NH)
    def _(i):
        halo_copy(i).wait_send()
        return_copy(i).wait_send()

    @pl.loop(0, NP)
    def _(block):
        given(dq_parts(block))
        given(dkv_parts(block))

    for away, stay in out_copies:
        away.wait()
        stay.wait()

    for dz in range(1, NZ):
        slot = (z + dz) % NZ
        pltpu.make_async_copy(ar_b.at[slot], ar_b.at[slot], arb_recv.at[slot]).wait()
    gains = jnp.sum(ar_b[...], axis=0)
    qterm_out[...] = gains[0:1]
    kterm_out[...] = gains[1:2]


def deliver(*refs):
    n = (len(refs) - 1) // 2
    copies = [pltpu.make_async_copy(refs[i], refs[n + i], refs[-1].at[i]) for i in range(n)]
    for copy in copies:
        copy.start()
    for copy in copies:
        copy.wait()


def per_device(query_input, key_input, saved_value_input, grad_output, query_gain, key_gain):
    frequency = (10000.0 ** (-np.arange(64, dtype=np.float64) / 64)).astype(np.float32)
    frequency = jnp.asarray(np.concatenate([frequency, frequency])[None, :])
    vmem = pl.BlockSpec(memory_space=pltpu.VMEM)
    dma = pltpu.SemaphoreType.DMA
    regular = pltpu.SemaphoreType.REGULAR
    span = (NP + NH) * T
    held = pl.BlockSpec(memory_space=pltpu.HBM)
    shapes = (
        jax.ShapeDtypeStruct((T, 16 * D), BF16),
        jax.ShapeDtypeStruct((T, 8 * D), BF16),
        jax.ShapeDtypeStruct((T, 8 * D), BF16),
        jax.ShapeDtypeStruct((1, D), F32),
        jax.ShapeDtypeStruct((1, D), F32),
    )
    results = pl.pallas_call(
        kernel,
        out_shape=tuple(pltpu.VMEM(sh.shape, sh.dtype) for sh in shapes),
        in_specs=[held] * 7,
        out_specs=(vmem,) * 5,
        scratch_shapes=[
            pltpu.VMEM((1, D), F32),
            pltpu.VMEM((1, D), F32),
            pltpu.VMEM((1, D), F32),
            pltpu.VMEM((2, T, 4 * D), BF16),
            pltpu.VMEM((2, T, 8 * D), BF16),
            pltpu.VMEM((2, span, D), BF16),
            pltpu.VMEM((2, NP * T, 2 * D), BF16),
            pltpu.VMEM((span, D), BF16),
            pltpu.VMEM((span, D), F32),
            pltpu.VMEM((D, span), BF16),
            pltpu.VMEM((span, D), F32),
            pltpu.VMEM((span, D), F32),
            pltpu.VMEM((2, (NH + 1) * T, 2 * T), F32),
            pltpu.VMEM((2, (NH + 1) * T, 2 * T), F32),
            pltpu.VMEM((2, (NH + 1) * T, 2 * T), BF16),
            pltpu.VMEM((2, (NH + 1) * T, 2 * T), BF16),
            pltpu.VMEM((2, span, D), F32),
            pltpu.VMEM((NP, T, 2 * D), BF16),
            pltpu.VMEM((NP, 2, T, D), BF16),
            pltpu.VMEM((NH, 2, T, D), BF16),
            pltpu.VMEM((NH, 2, T, D), BF16),
            pltpu.VMEM((2, T, 8 * D), BF16),
            pltpu.VMEM((2, 2, T, 4 * D), BF16),
            pltpu.VMEM((8, D), F32),
            pltpu.VMEM((NP, 8, D), F32),
            pltpu.VMEM((NZ, 8, D), F32),
            pltpu.VMEM((NX, 8, D), F32),
            dma((4,)),
            dma((4,)),
            dma((2, 2, 4)),
            dma((2, NP)),
            dma((2, 2, 4)),
            dma((2, NP)),
            dma((NH,)),
            dma((NH,)),
            dma((NH,)),
            dma((NH,)),
            dma((NP,)),
            dma((4, 2)),
            dma((NP,)),
            dma((4, 2)),
            dma((3,)),
            dma((3,)),
            dma((3,)),
            dma((NP,)),
            dma((NP,)),
            dma((NZ,)),
            dma((NZ,)),
            dma((NX,)),
            dma((NX,)),
            dma((3,)),
            regular,
            regular,
            regular,
            regular,
        ],
        compiler_params=pltpu.CompilerParams(
            collective_id=0, has_side_effects=True, vmem_limit_bytes=61 * 2**20
        ),
        cost_estimate=pl.CostEstimate(flops=1700000000, bytes_accessed=3000000, transcendentals=1400000),
    )(
        query_input,
        key_input,
        saved_value_input,
        grad_output,
        query_gain.reshape(1, D),
        key_gain.reshape(1, D),
        frequency,
    )
    dq, dk, dv, qterm, kterm = pl.pallas_call(
        deliver,
        out_shape=shapes,
        in_specs=[pl.BlockSpec(memory_space=pl.ANY)] * 5,
        out_specs=(held,) * 5,
        scratch_shapes=[dma((5,))],
        compiler_params=pltpu.CompilerParams(vmem_limit_bytes=2**20),
    )(*results)
    return dq, dk, dv, qterm.reshape(D), kterm.reshape(D)


def solution(mesh):
    tokens = P(("seq", "sub"), None)
    return jax.shard_map(
        per_device,
        mesh=mesh,
        in_specs=(tokens, tokens, tokens, tokens, P(), P()),
        out_specs=(tokens, tokens, tokens, P(), P()),
        check_vma=False,
    )
```

```python
import functools

import jax
import jax.numpy as jnp
import numpy as np
from jax import lax
from jax.experimental import pallas as pl
from jax.experimental.pallas import tpu as pltpu
from jax.sharding import PartitionSpec as P

MESH = pl.DeviceIdType.MESH
T = 128
D = 128
NP = 8
NH = 4
NZ = 16
NX = 4
EPS = 1e-6
SCALE = 168.0 ** (-0.5)
LOG2E = 1.4426950408889634
LN2 = 0.6931471805599453
F32 = jnp.float32
BF16 = jnp.bfloat16


def device(col, y, c):
    return ((col * 2 + y // 2) * 2 + c, y % 2)


def place(y, c):
    return 4 * (y // 2) + 2 * c + y % 2


def rows_of(block, blocks=1):
    return pl.ds(pl.multiple_of(block * T, T), blocks * T)


def cols_of(start, size):
    return pl.ds(pl.multiple_of(start, 128), size)


def unit_of(raw):
    inverse = lax.rsqrt(jnp.mean(raw * raw, axis=-1, keepdims=True) + EPS)
    return raw * inverse, inverse


def rope(rows, cosine, sine):
    return rows * cosine + pltpu.roll(rows, 64, 1) * sine


def rope_back(rows, cosine, sine):
    return rows * cosine - pltpu.roll(rows, 64, 1) * sine


def dot_nt(a, b):
    return lax.dot_general(a, b, (((1,), (1,)), ((), ())), preferred_element_type=F32)


def dot_nn(a, b):
    return jnp.dot(a, b, preferred_element_type=F32)


def kernel(
    q_in,
    k_in,
    v_in,
    g_in,
    qgain_in,
    kgain_in,
    freq_in,
    dq_out,
    dk_out,
    dv_out,
    qterm_out,
    kterm_out,
    qgain_ref,
    kgain_ref,
    freq_ref,
    st_kv,
    st_qg,
    kv,
    qg,
    kready,
    kunit,
    ktrans,
    ctab,
    stab,
    weights,
    gprobs,
    probs_low,
    grad_scores,
    dkv,
    dq_res,
    dkv_res,
    halo_res,
    halo_ret,
    plane_q,
    plane_kv,
    terms,
    ar_a,
    ar_b,
    ar_c,
    core_send,
    core_recv,
    kv_send,
    kv_recv,
    qg_send,
    qg_recv,
    halo_send,
    halo_recv,
    ret_send,
    ret_recv,
    dq_send,
    dq_recv,
    dkv_send,
    dkv_recv,
    out_send,
    out_recv,
    out_local,
    ara_send,
    ara_recv,
    arb_send,
    arb_recv,
    arc_send,
    arc_recv,
    small_sem,
    relay_up,
    relay_one,
    relay_two,
    relay_four,
):
    s = lax.axis_index("seq")
    c = s % 2
    col = s // 4
    y = 2 * ((s // 2) % 2) + lax.axis_index("sub")
    z = col % NZ
    x = col // NZ
    other = 1 - c
    mine = place(y, c)
    theirs = place(y, other)
    partner = device(col, y, other)
    after = device((col + 1) % (NX * NZ), y, c)
    before = device((col + NX * NZ - 1) % (NX * NZ), y, c)

    column_peers = [(dy, dc) for dy in range(4) for dc in range(2) if (dy, dc) != (0, 0)]

    def column_device(dy, dc):
        return device(col, (y + dy) % 4, (c + dc) % 2)

    def z_device(dz):
        return device(x * NZ + (z + dz) % NZ, y, c)

    def x_device(dx):
        return device(((x + dx) % NX) * NZ + z, y, c)

    def greet(semaphore, target):
        pl.semaphore_signal(semaphore, inc=1, device_id=target, device_id_type=MESH)

    def load_small(i):
        src, dst = ((qgain_in, qgain_ref), (kgain_in, kgain_ref), (freq_in, freq_ref))[i]
        return pltpu.make_async_copy(src, dst, small_sem.at[i])

    for i in range(3):
        load_small(i).start()

    barrier = pltpu.get_barrier_semaphore()
    greeted = [column_device(dy, dc) for dy, dc in column_peers]
    greeted += [before, z_device(NZ - 1), x_device(NX - 1)]
    for target in greeted:
        greet(barrier, target)
    pl.semaphore_wait(barrier, len(greeted))
    greet(relay_up, z_device(1))
    greet(relay_up, x_device(1))

    def remote(src, dst, send, recv, target):
        return pltpu.make_async_remote_copy(
            src_ref=src, dst_ref=dst, send_sem=send, recv_sem=recv, device_id=target, device_id_type=MESH
        )

    sends = []

    core_copies = []
    for i, (ref, width) in enumerate(((k_in, 4 * D), (v_in, 4 * D), (q_in, 8 * D), (g_in, 8 * D))):
        stage = st_kv.at[i] if i < 2 else st_qg.at[i - 2]
        core_copies.append(
            remote(ref.at[:, cols_of(other * width, width)], stage, core_send.at[i], core_recv.at[i], partner)
        )

    def spread(kind, sources, width, slots, first_row_block, send, recv, block, turn):
        for i, source in enumerate(sources):
            base, ref = source
            for dy in range(1, 4):
                yy = (y + dy) % 4
                copy = remote(
                    ref.at[:, cols_of(base + yy * width, width)],
                    slots.at[i, rows_of(first_row_block + block)],
                    send.at[turn, i, dy],
                    recv.at[i, block],
                    device(col, yy, c),
                )
                copy.start()
                sends.append(copy)
            pltpu.make_async_copy(
                ref.at[:, cols_of(base + y * width, width)],
                slots.at[i, rows_of(first_row_block + block)],
                recv.at[i, block],
            ).start()

    core_copies[0].start()
    core_copies[1].start()
    own_kv = [(c * 4 * D, k_in), (c * 4 * D, v_in)]
    spread("kv", own_kv, D, kv, NH, kv_send, kv_recv, mine, 0)
    core_copies[2].start()
    core_copies[3].start()
    core_copies[0].wait_recv()
    core_copies[1].wait_recv()
    spread("kv", [(0, st_kv.at[0]), (0, st_kv.at[1])], D, kv, NH, kv_send, kv_recv, theirs, 1)
    own_qg = [(c * 8 * D, q_in), (c * 8 * D, g_in)]
    spread("qg", own_qg, 2 * D, qg, 0, qg_send, qg_recv, mine, 0)
    core_copies[2].wait_recv()
    core_copies[3].wait_recv()
    spread("qg", [(0, st_qg.at[0]), (0, st_qg.at[1])], 2 * D, qg, 0, qg_send, qg_recv, theirs, 1)

    for i in range(3):
        load_small(i).wait()

    first_token = col * (NP * T) - NH * T
    half = (NP + NH) * T // 2
    step_rows = 64

    @pl.loop(0, half // step_rows)
    def _(step):
        row = lax.broadcasted_iota(jnp.int32, (step_rows, D), 0)
        lane = lax.broadcasted_iota(jnp.int32, (step_rows, D), 1)
        low = lane < 64
        token = first_token + step * step_rows + row + jnp.where(low, 0, half)
        angle = token.astype(F32) * freq_ref[...]
        cosine = jnp.cos(angle)
        sine = jnp.sin(angle)
        cosine_turned = pltpu.roll(cosine, 64, 1)
        sine_turned = pltpu.roll(sine, 64, 1)
        near = pl.ds(pl.multiple_of(step * step_rows, step_rows), step_rows)
        far = pl.ds(pl.multiple_of(half + step * step_rows, step_rows), step_rows)
        ctab[near] = jnp.where(low, cosine, cosine_turned)
        ctab[far] = jnp.where(low, cosine_turned, cosine)
        stab[near] = jnp.where(low, -sine, sine_turned)
        stab[far] = jnp.where(low, -sine_turned, sine)

    dkv[...] = jnp.zeros_like(dkv)
    terms[...] = jnp.zeros_like(terms)
    kgain = kgain_ref[...]
    qgain = qgain_ref[...]

    def wait_kv(block):
        for i in range(2):
            slot = kv.at[i, rows_of(NH + block)]
            pltpu.make_async_copy(slot, slot, kv_recv.at[i, block]).wait()

    def halo_copy(i):
        return remote(
            kv.at[:, rows_of(NP + i)], kv.at[:, rows_of(i)], halo_send.at[i], halo_recv.at[i], after
        )

    def prepare_keys(block):
        rows = rows_of(block, NH)
        unit, _ = unit_of(kv[0, rows].astype(F32))
        turned = rope(unit * kgain, ctab[rows], stab[rows])
        kunit[rows] = unit
        kready[rows] = turned.astype(BF16)
        ktrans[:, cols_of(block * T, NH * T)] = turned.T.astype(BF16)

    @pl.loop(0, NH)
    def _(turn):
        core = turn // 2 + c - 2 * (turn // 2) * c
        i = 2 * core + turn % 2
        wait_kv(NH + i)
        halo_copy(i).start()

    pl.semaphore_wait(relay_up, 2)
    for target in (z_device(1), z_device(NZ - 1), x_device(1), x_device(NX - 1)):
        greet(relay_one, target)

    @pl.loop(0, NH)
    def _(i):
        wait_kv(i)

    prepare_keys(NH)
    prepare_keys(2 * NH)

    pl.semaphore_wait(relay_one, 4)
    greet(relay_two, z_device(2))
    greet(relay_two, z_device(NZ - 2))

    halo_valid = jnp.where(col == 0, 0.0, 1.0)
    key_row = lax.broadcasted_iota(jnp.int32, (T, 2 * T), 0)
    query_lane = lax.broadcasted_iota(jnp.int32, (T, 2 * T), 1) % T
    newer = key_row > query_lane

    def norm_back(turned_grad, raw, gain, cosine, sine):
        unit, inverse = unit_of(raw)
        w = rope_back(turned_grad, cosine, sine)
        term = jnp.sum(w * unit, axis=0, keepdims=True)
        grad_unit = w * gain
        grad = (grad_unit - unit * jnp.mean(grad_unit * unit, axis=-1, keepdims=True)) * inverse
        return grad.astype(BF16), term

    def owner(block):
        return 2 * (block // 4) + block % 2, (block // 2) % 2

    def dq_parts(block):
        yy, cc = owner(block)
        return dq_res.at[block], plane_q.at[cc, :, cols_of(y * 2 * D, 2 * D)], dq_send.at[block], dq_recv.at[y, cc], yy

    def dkv_parts(block):
        yy, cc = owner(block)
        return dkv_res.at[block], plane_kv.at[cc, :, :, cols_of(y * D, D)], dkv_send.at[block], dkv_recv.at[y, cc], yy

    def give(parts):
        src, dst, send, recv, yy = parts

        @pl.when(yy == y)
        def _():
            pltpu.make_async_copy(src, dst, recv).start()

        @pl.when(yy != y)
        def _():
            remote(src, dst, send, recv, device(col, yy, c)).start()

    def given(parts):
        src, dst, send, recv, yy = parts

        @pl.when(yy != y)
        def _():
            remote(src, dst, send, recv, device(col, yy, c)).wait_send()

    def attend(first_block):
        blocks = [first_block, first_block + 1]
        for block in blocks:
            for i in range(2):
                slot = qg.at[i, rows_of(block)]
                pltpu.make_async_copy(slot, slot, qg_recv.at[i, block]).wait()
        raws, queries, grads, turns = [], [], [], []
        for block in blocks:
            rows, own = rows_of(block), rows_of(block + NH)
            cosine, sine = ctab[own], stab[own]
            raw = [qg[0, rows, h * D : (h + 1) * D].astype(F32) for h in range(2)]
            turned = [(rope(unit_of(r)[0] * qgain, cosine, sine) * (SCALE * LOG2E)).astype(BF16) for r in raw]
            raws.append(raw)
            turns.append((cosine, sine))
            queries.append(jnp.concatenate(turned, axis=0))
            grads.append(jnp.concatenate([qg[1, rows, h * D : (h + 1) * D] for h in range(2)], axis=0))
        for n, block in enumerate(blocks):
            window = rows_of(block, NH + 1)
            weights[n] = dot_nt(kready[window], queries[n])
            gprobs[n] = dot_nt(kv[1, window], grads[n])
        sums = []
        for n, block in enumerate(blocks):
            total = jnp.zeros((1, 2 * T), F32)
            inner = jnp.zeros((1, 2 * T), F32)
            for t in range(NH + 1):
                part = slice(t * T, (t + 1) * T)
                weight = jnp.exp2(weights[n, part])
                if t == 0:
                    weight = jnp.where(newer, weight, 0.0)
                if t == NH:
                    weight = jnp.where(newer, 0.0, weight)
                else:
                    weight = weight * jnp.where(block + t < NH, halo_valid, 1.0)
                total = total + jnp.sum(weight, axis=0, keepdims=True)
                inner = inner + jnp.sum(weight * gprobs[n, part], axis=0, keepdims=True)
                weights[n, part] = weight
            inverse = 1.0 / total
            sums.append((inverse, inner * inverse))
        for n, block in enumerate(blocks):
            inverse, inner = sums[n]
            for t in range(NH + 1):
                part = slice(t * T, (t + 1) * T)
                prob = weights[n, part] * inverse
                probs_low[n, part] = prob.astype(BF16)
                grad_scores[n, part] = (prob * (gprobs[n, part] - inner)).astype(BF16)
        grad_query = [
            dot_nn(ktrans[:, cols_of(block * T, (NH + 1) * T)], grad_scores[n]) for n, block in enumerate(blocks)
        ]
        for n, block in enumerate(blocks):
            window = rows_of(block, NH + 1)
            dkv[1, window] += dot_nn(probs_low[n], grads[n])
            dkv[0, window] += dot_nn(grad_scores[n], queries[n])
        terms_here = jnp.zeros((1, D), F32)
        for n, block in enumerate(blocks):
            for h in range(2):
                turned = grad_query[n][:, h * T : (h + 1) * T].T * SCALE
                grad, term = norm_back(turned, raws[n][h], qgain, *turns[n])
                dq_res[block, :, h * D : (h + 1) * D] = grad
                terms_here = terms_here + term
        terms[0:1] += terms_here

    late = jnp.where(z == 0, 1, 0)
    halo_turn = 1 + late

    @pl.loop(0, NP // 2)
    def _(i):
        @pl.when(i == halo_turn)
        def _():
            @pl.loop(0, NH)
            def _(j):
                halo_copy(j).wait_recv()

            prepare_keys(0)

            pl.semaphore_wait(relay_two, 2)
            greet(relay_four, z_device(4))
            greet(relay_four, z_device(NZ - 4))

        major, minor = i // 2, i % 2
        first = late * major + (1 - late) * minor
        swapped = late * minor + (1 - late) * major
        core = swapped + c - 2 * swapped * c
        block = 4 * (1 - first) + 2 * core
        attend(block)
        give(dq_parts(block))
        give(dq_parts(block + 1))

    def return_copy(i):
        return remote(halo_res.at[i], halo_ret.at[i], ret_send.at[i], ret_recv.at[i], before)

    @pl.loop(0, NH)
    def _(block):
        keys = rows_of(block)
        halo_res[block, 0] = (dkv[0, keys] * LN2).astype(BF16)
        halo_res[block, 1] = dkv[1, keys].astype(BF16)
        return_copy(block).start()

    @pl.loop(0, (NH + NP) // NH)
    def _(part):
        keys = rows_of(part * NH, NH)
        w = rope_back(dkv[0, keys] * LN2, ctab[keys], stab[keys])
        terms[1:2] += jnp.sum(w * kunit[keys], axis=0, keepdims=True)

    ar_a[mine] = terms[...]
    stage_a = [
        remote(terms, ar_a.at[mine], ara_send.at[i], ara_recv.at[mine], column_device(dy, dc))
        for i, (dy, dc) in enumerate(column_peers)
    ]
    for copy in stage_a:
        copy.start()

    for dy, dc in column_peers:
        slot = place((y + dy) % 4, (c + dc) % 2)
        pltpu.make_async_copy(ar_a.at[slot], ar_a.at[slot], ara_recv.at[slot]).wait()
    ar_c[x] = jnp.sum(ar_a[...], axis=0)
    stage_c = [
        remote(ar_c.at[x], ar_c.at[x], arc_send.at[dx], arc_recv.at[x], x_device(dx)) for dx in range(1, NX)
    ]
    for copy in stage_c:
        copy.start()


    keys = rows_of(NH, NH)
    grad, _ = norm_back(dkv[0, keys] * LN2, kv[0, keys].astype(F32), kgain, ctab[keys], stab[keys])
    dkv_res[0:NH, 0] = grad.reshape(NH, T, D)
    dkv_res[0:NH, 1] = dkv[1, keys].astype(BF16).reshape(NH, T, D)

    @pl.loop(0, NH)
    def _(block):
        give(dkv_parts(block))

    pl.semaphore_wait(relay_four, 2)
    for dx in range(1, NX):
        slot = (x + dx) % NX
        pltpu.make_async_copy(ar_c.at[slot], ar_c.at[slot], arc_recv.at[slot]).wait()
    ar_b[z] = jnp.sum(ar_c[...], axis=0)
    farthest_first = sorted(range(1, NZ), key=lambda dz: abs(dz - NZ // 2))
    stage_b = [
        remote(ar_b.at[z], ar_b.at[z], arb_send.at[dz], arb_recv.at[z], z_device(dz)) for dz in farthest_first
    ]
    for copy in stage_b:
        copy.start()

    @pl.loop(NH, NP)
    def _(block):
        return_copy(block - NH).wait_recv()
        keys = rows_of(block + NH)
        grad_key = dkv[0, keys] * LN2 + halo_ret[block - NH, 0].astype(F32)
        grad, _ = norm_back(grad_key, kv[0, keys].astype(F32), kgain, ctab[keys], stab[keys])
        dkv_res[block, 0] = grad
        dkv_res[block, 1] = (dkv[1, keys] + halo_ret[block - NH, 1].astype(F32)).astype(BF16)
        give(dkv_parts(block))

    wide, narrow = cols_of(c * 8 * D, 8 * D), cols_of(c * 4 * D, 4 * D)
    plane_parts = (
        (lambda cc: plane_q.at[cc], dq_out.at[:, wide]),
        (lambda cc: plane_kv.at[cc, 0], dk_out.at[:, narrow]),
        (lambda cc: plane_kv.at[cc, 1], dv_out.at[:, narrow]),
    )
    out_copies = []
    for i, (part, target) in enumerate(plane_parts):
        if i < 2:
            for cc in range(2):
                for yy in range(4):
                    if i == 0:
                        slot = plane_q.at[cc, :, cols_of(yy * 2 * D, 2 * D)]
                        sem = dq_recv.at[yy, cc]
                    else:
                        slot = plane_kv.at[cc, :, :, cols_of(yy * D, D)]
                        sem = dkv_recv.at[yy, cc]
                    pltpu.make_async_copy(slot, slot, sem).wait()
        away = remote(part(other), target, out_send.at[i], out_recv.at[i], partner)
        stay = pltpu.make_async_copy(part(c), target, out_local.at[i])
        away.start()
        stay.start()
        out_copies.append((away, stay))

    for copy in core_copies + sends + stage_a + stage_b + stage_c:
        copy.wait_send()

    @pl.loop(0, NH)
    def _(i):
        halo_copy(i).wait_send()
        return_copy(i).wait_send()

    @pl.loop(0, NP)
    def _(block):
        given(dq_parts(block))
        given(dkv_parts(block))

    for away, stay in out_copies:
        away.wait()
        stay.wait()

    for dz in range(1, NZ):
        slot = (z + dz) % NZ
        pltpu.make_async_copy(ar_b.at[slot], ar_b.at[slot], arb_recv.at[slot]).wait()
    gains = jnp.sum(ar_b[...], axis=0)
    qterm_out[...] = gains[0:1]
    kterm_out[...] = gains[1:2]


def deliver(*refs):
    n = (len(refs) - 1) // 2
    copies = [pltpu.make_async_copy(refs[i], refs[n + i], refs[-1].at[i]) for i in range(n)]
    for copy in copies:
        copy.start()
    for copy in copies:
        copy.wait()


def per_device(query_input, key_input, saved_value_input, grad_output, query_gain, key_gain):
    frequency = (10000.0 ** (-np.arange(64, dtype=np.float64) / 64)).astype(np.float32)
    frequency = jnp.asarray(np.concatenate([frequency, frequency])[None, :])
    vmem = pl.BlockSpec(memory_space=pltpu.VMEM)
    dma = pltpu.SemaphoreType.DMA
    regular = pltpu.SemaphoreType.REGULAR
    span = (NP + NH) * T
    held = pl.BlockSpec(memory_space=pltpu.HBM)
    shapes = (
        jax.ShapeDtypeStruct((T, 16 * D), BF16),
        jax.ShapeDtypeStruct((T, 8 * D), BF16),
        jax.ShapeDtypeStruct((T, 8 * D), BF16),
        jax.ShapeDtypeStruct((1, D), F32),
        jax.ShapeDtypeStruct((1, D), F32),
    )
    results = pl.pallas_call(
        kernel,
        out_shape=tuple(pltpu.VMEM(sh.shape, sh.dtype) for sh in shapes),
        in_specs=[held] * 7,
        out_specs=(vmem,) * 5,
        scratch_shapes=[
            pltpu.VMEM((1, D), F32),
            pltpu.VMEM((1, D), F32),
            pltpu.VMEM((1, D), F32),
            pltpu.VMEM((2, T, 4 * D), BF16),
            pltpu.VMEM((2, T, 8 * D), BF16),
            pltpu.VMEM((2, span, D), BF16),
            pltpu.VMEM((2, NP * T, 2 * D), BF16),
            pltpu.VMEM((span, D), BF16),
            pltpu.VMEM((span, D), F32),
            pltpu.VMEM((D, span), BF16),
            pltpu.VMEM((span, D), F32),
            pltpu.VMEM((span, D), F32),
            pltpu.VMEM((2, (NH + 1) * T, 2 * T), F32),
            pltpu.VMEM((2, (NH + 1) * T, 2 * T), F32),
            pltpu.VMEM((2, (NH + 1) * T, 2 * T), BF16),
            pltpu.VMEM((2, (NH + 1) * T, 2 * T), BF16),
            pltpu.VMEM((2, span, D), F32),
            pltpu.VMEM((NP, T, 2 * D), BF16),
            pltpu.VMEM((NP, 2, T, D), BF16),
            pltpu.VMEM((NH, 2, T, D), BF16),
            pltpu.VMEM((NH, 2, T, D), BF16),
            pltpu.VMEM((2, T, 8 * D), BF16),
            pltpu.VMEM((2, 2, T, 4 * D), BF16),
            pltpu.VMEM((8, D), F32),
            pltpu.VMEM((NP, 8, D), F32),
            pltpu.VMEM((NZ, 8, D), F32),
            pltpu.VMEM((NX, 8, D), F32),
            dma((4,)),
            dma((4,)),
            dma((2, 2, 4)),
            dma((2, NP)),
            dma((2, 2, 4)),
            dma((2, NP)),
            dma((NH,)),
            dma((NH,)),
            dma((NH,)),
            dma((NH,)),
            dma((NP,)),
            dma((4, 2)),
            dma((NP,)),
            dma((4, 2)),
            dma((3,)),
            dma((3,)),
            dma((3,)),
            dma((NP,)),
            dma((NP,)),
            dma((NZ,)),
            dma((NZ,)),
            dma((NX,)),
            dma((NX,)),
            dma((3,)),
            regular,
            regular,
            regular,
            regular,
        ],
        compiler_params=pltpu.CompilerParams(
            collective_id=0, has_side_effects=True, vmem_limit_bytes=61 * 2**20
        ),
        cost_estimate=pl.CostEstimate(flops=1700000000, bytes_accessed=3000000, transcendentals=1400000),
    )(
        query_input,
        key_input,
        saved_value_input,
        grad_output,
        query_gain.reshape(1, D),
        key_gain.reshape(1, D),
        frequency,
    )
    dq, dk, dv, qterm, kterm = pl.pallas_call(
        deliver,
        out_shape=shapes,
        in_specs=[pl.BlockSpec(memory_space=pl.ANY)] * 5,
        out_specs=(held,) * 5,
        scratch_shapes=[dma((5,))],
        compiler_params=pltpu.CompilerParams(vmem_limit_bytes=2**20),
    )(*results)
    return dq, dk, dv, qterm.reshape(D), kterm.reshape(D)


def solution(mesh):
    tokens = P(("seq", "sub"), None)
    return jax.shard_map(
        per_device,
        mesh=mesh,
        in_specs=(tokens, tokens, tokens, tokens, P(), P()),
        out_specs=(tokens, tokens, tokens, P(), P()),
        check_vma=False,
    )
```
